256 devices in a mesh: seq: 64 (over x, z_hi, y, core), chan: 4 (over z_lo).
Axes of the slice: x: 4, y: 4, z: 8 (z_hi: 2, z_lo: 4; z = z_hi * 4 + z_lo), core: 2. Of those that a mesh axis runs over, the one named last changes fastest.
Arguments:
- values: bfloat16 [8192, 4096], P('seq', 'chan'), may hold values from -6 to 6
- gates: bfloat16 [8192, 4096], P('seq', 'chan'), may hold values from -6 to 6
- grad_out: float32 [8192, 4096], P('seq', 'chan'), may hold values from -6 to 6
- filter_raw: bfloat16 [8192, 1024], P('seq'), may hold values from -6 to 6
- skip_gain: float32 [4096], P('chan'), may hold values from 0.5 to 1.5
Outputs:
- value_grad: bfloat16 [8192, 4096], P('seq', 'chan')
- gate_grad: bfloat16 [8192, 4096], P('seq', 'chan')
- filter_grad: float32 [8192, 1024], P('seq', 'chan')
The draws below stay inside these ranges and needn't reach their ends.
All inputs are finite; a program needn't handle non-finite values.
Results may differ from the reference program's by a relative error of at most 0.01.
Values may be sent and summed in bfloat16 or wider, within the bound.
No kernel may reach another device: no remote copies, remote signals or barrier semaphores. Data moves between devices by JAX's collectives and lax.ppermute only.
A program may use at most 64 MiB of HBM per device.

```python
import math
import jax
import jax.numpy as jnp
from jax import lax

D_SLAB = 4096
SEQ = 8192
FILTERS = 1024


def shard_levels(stream_key, extent, cuts, low, top_value):
    def one(dim, shards_of):
        draws = jax.random.uniform(jax.random.fold_in(jax.random.fold_in(stream_key, 6), dim), (shards_of,), jnp.float32, low / len(cuts), top_value / len(cuts))
        return jnp.repeat(jnp.exp(draws), extent[dim] // shards_of).reshape((-1,) + (1,) * (len(extent) - dim - 1))

    level = one(*cuts[0])
    for cut in cuts[1:]:
        level = level * one(*cut)
    return level


def bell_draw(key, extent, scale, limit, split=(), dtype=jnp.bfloat16):
    gain = shard_levels(key, extent, split, -0.22, 0.18) if split else 1.0
    result = jax.random.normal(key, extent, jnp.float32) * scale * gain
    return jnp.minimum(jnp.maximum(result, -limit), limit).astype(dtype)


def setup_inputs(seed: int = 0) -> dict:
    streams_of = jax.random.split(jax.random.key(seed), 6)
    return {
        "values": bell_draw(streams_of[0], (SEQ, D_SLAB), 1.0, 6.0, ((0, 64), (1, 4))),
        "gates": bell_draw(streams_of[1], (SEQ, D_SLAB), 1.0, 6.0, ((0, 64), (1, 4))),
        "grad_out": bell_draw(streams_of[2], (SEQ, D_SLAB), 1.0, 6.0, ((0, 64), (1, 4)), jnp.float32),
        "filter_raw": bell_draw(streams_of[3], (SEQ, FILTERS), 1.0, 6.0, ((0, 64),)),
        "skip_gain": jnp.clip(0.5 + 1.0 * jax.random.uniform(streams_of[4], (D_SLAB,), jnp.float32) ** shard_levels(streams_of[4], (D_SLAB,), ((0, 4),), -0.2, 0.2), 0.5, 1.5),
    }


def block_grads(values, gates, grad_out, filters, skip_gain):
    length = values.shape[0]
    period = 2 * length
    scale = 1.0 / math.sqrt(length)
    gate_term = (grad_out * gates.astype(jnp.float32)).astype(jnp.bfloat16)
    gate_wide = gate_term.astype(jnp.float32)
    value_wide = values.astype(jnp.float32)
    spec_values = jnp.fft.rfft(value_wide, n=period, axis=0)
    spec_filter = jnp.fft.rfft(filters.astype(jnp.float32), n=period, axis=0)
    spec_gate = jnp.fft.rfft(gate_wide, n=period, axis=0)
    conv = jnp.fft.irfft(spec_filter * spec_values, n=period, axis=0)[:length] * scale
    back_v = jnp.fft.irfft(jnp.conj(spec_filter) * spec_gate, n=period, axis=0)[:length] * scale
    back_h = jnp.fft.irfft(jnp.conj(spec_values) * spec_gate, n=period, axis=0)[:length] * scale
    mixed = conv + skip_gain * value_wide
    gate_grad = (grad_out * mixed).astype(jnp.bfloat16)
    value_grad = (back_v + skip_gain * gate_wide).astype(jnp.bfloat16)
    return (value_grad, gate_grad, back_h.astype(jnp.float32))

def reference(values, gates, grad_out, filter_raw, skip_gain):
    copies = D_SLAB // FILTERS
    filters = jnp.tile(filter_raw, (1, copies))
    width = 128 if D_SLAB % 128 == 0 else D_SLAB
    groups = D_SLAB // width

    def split_cols(array):
        return jnp.moveaxis(array.reshape(SEQ, groups, width), 1, 0)

    def join_cols(array):
        return jnp.moveaxis(array, 0, 1).reshape(SEQ, D_SLAB)
    results = lax.map(lambda items: block_grads(*items), (split_cols(values), split_cols(gates), split_cols(grad_out), split_cols(filters), skip_gain.reshape(groups, 1, width)))
    value_grad = join_cols(results[0])
    gate_grad = join_cols(results[1])
    filter_grad = lax.optimization_barrier(jnp.sum(join_cols(results[2]).reshape(SEQ, copies, FILTERS), axis=1))
    return (value_grad, gate_grad, filter_grad)
```

```python
import math

import jax
import jax.numpy as jnp
import numpy as np
from jax import lax
from jax.experimental import pallas as pl
from jax.experimental.pallas import tpu as pltpu
from jax.sharding import PartitionSpec as P

F32 = jnp.float32
BF16 = jnp.bfloat16
VMEM = pl.BlockSpec(memory_space=pltpu.VMEM)


def split_pair(table):
    high = table.astype(np.float32).astype(jnp.bfloat16)
    low = (table - high.astype(np.float64)).astype(np.float32).astype(jnp.bfloat16)
    return high, low


def tables(blocks, rows):
    period = 2 * blocks * rows
    scale = 2.0 / period / math.sqrt(blocks * rows)
    half = np.arange(blocks) + 0.5
    block_angle = 2.0 * np.pi / (2 * blocks) * np.outer(half, np.arange(blocks))
    enter = np.concatenate([np.cos(block_angle), -np.sin(block_angle)], axis=0)
    leave = np.concatenate([np.cos(block_angle), -np.sin(block_angle)], axis=0).T * scale
    turn = 2.0 * np.pi / period * np.outer(half, np.arange(rows))
    row_angle = 2.0 * np.pi / rows * np.outer(np.arange(rows), np.arange(rows))
    row_cos, row_sin = np.cos(row_angle), np.sin(row_angle)
    forward = np.block([[row_cos, -row_sin], [row_sin, row_cos]])
    inverse = np.block([[row_cos, row_sin], [-row_sin, row_cos]])
    enter_pair = np.concatenate(split_pair(enter), axis=0)
    leave_high, leave_low = split_pair(leave)
    leave_pair = np.concatenate([leave_high, leave_low], axis=0)
    return (
        enter_pair,
        leave_pair,
        *split_pair(forward),
        *split_pair(inverse),
        np.cos(turn).astype(np.float32),
        np.sin(turn).astype(np.float32),
    )


def split_value(x):
    high = x.astype(BF16)
    return high, (x - high.astype(F32)).astype(BF16)


def dot(a, b):
    return jnp.dot(a, b, preferred_element_type=F32)


def dot_wide(x, high, low):
    x_high, x_low = split_value(x)
    return dot(x_high, high) + (dot(x_low, high) + dot(x_high, low))


def pack_kernel(values_ref, gates_ref, grad_ref, filter_ref, out_ref):
    group = out_ref.shape[1] // 3
    parts = (
        values_ref[...].astype(F32),
        (grad_ref[...] * gates_ref[...].astype(F32)).astype(BF16).astype(F32),
        filter_ref[...].astype(F32),
    )
    for a, part in enumerate(parts):
        turned = part.T.astype(BF16)
        out_ref[:, a * group : (a + 1) * group, :] = turned.reshape(-1, group, part.shape[0])


def spectra_kernel(
    in_ref, enter_ref, leave_ref, fwd_h, fwd_l, inv_h, inv_l, cos_ref, sin_ref, out_ref, wide, result
):
    blocks, rows = in_ref.shape[0], in_ref.shape[2]
    group = in_ref.shape[1] // 3
    step = 4
    for a in range(3):
        part = in_ref[:, a * group : (a + 1) * group, :]
        wide[a] = part.astype(F32).reshape(blocks * group, rows)
    cos_t, sin_t = cos_ref[...], sin_ref[...]

    def spectrum(a, c0):
        cols = [wide[a, pl.ds(c0 + c, blocks, stride=group), :] for c in range(step)]
        mixed = dot(enter_ref[...], jnp.concatenate(cols, axis=1).astype(BF16))
        mixed = mixed[: 2 * blocks] + mixed[2 * blocks :]
        turned = []
        for c in range(step):
            re = mixed[:blocks, c * rows : (c + 1) * rows]
            im = mixed[blocks:, c * rows : (c + 1) * rows]
            turned.append(
                jnp.concatenate([re * cos_t + im * sin_t, im * cos_t - re * sin_t], axis=1)
            )
        full = dot_wide(jnp.concatenate(turned, axis=0), fwd_h[...], fwd_l[...])
        return full[:, :rows], full[:, rows:]

    def signal(a, c0, re, im):
        full = dot_wide(jnp.concatenate([re, im], axis=1), inv_h[...], inv_l[...])
        cols = []
        for c in range(step):
            re = full[c * blocks : (c + 1) * blocks, :rows]
            im = full[c * blocks : (c + 1) * blocks, rows:]
            cols.append(
                jnp.concatenate([re * cos_t - im * sin_t, re * sin_t + im * cos_t], axis=0)
            )
        high, low = split_value(jnp.concatenate(cols, axis=1))
        pair = dot(leave_ref[...], high)
        mixed = pair[:blocks] + (pair[blocks:] + dot(leave_ref[:blocks, :], low))
        for c in range(step):
            result[a, pl.ds(c0 + c, blocks, stride=group), :] = mixed[:, c * rows : (c + 1) * rows]

    for c0 in range(0, group, step):
        v_re, v_im = spectrum(0, c0)
        g_re, g_im = spectrum(1, c0)
        h_re, h_im = spectrum(2, c0)
        signal(0, c0, h_re * v_re - h_im * v_im, h_re * v_im + h_im * v_re)
        signal(1, c0, h_re * g_re + h_im * g_im, h_re * g_im - h_im * g_re)
        signal(2, c0, v_re * g_re + v_im * g_im, v_re * g_im - v_im * g_re)
    for a in range(3):
        out_ref[:, a * group : (a + 1) * group, :] = (
            result[a].astype(BF16).reshape(blocks, group, rows)
        )


def finish_kernel(values_ref, gates_ref, grad_ref, skip_ref, in_ref, value_out, gate_out):
    group = in_ref.shape[1] // 3
    rows = in_ref.shape[2]

    def part(a):
        piece = in_ref[:, a * group : (a + 1) * group, :].astype(F32)
        return piece.reshape(-1, rows).T

    grad = grad_ref[...]
    skip = skip_ref[...]
    mixed = part(0) + skip * values_ref[...].astype(F32)
    gate_out[...] = (grad * mixed).astype(BF16)
    gate_term = (grad * gates_ref[...].astype(F32)).astype(BF16).astype(F32)
    value_out[...] = (part(1) + skip * gate_term).astype(BF16)


def sum_kernel(*refs):
    out_ref = refs[-1]
    rows = out_ref.shape[0]
    total = refs[0][...].astype(F32)
    for ref in refs[1:-1]:
        total = total + ref[...].astype(F32)
    out_ref[...] = total.reshape(-1, rows).T


def local(values, gates, grad_out, filter_raw, skip_gain):
    rows, width = values.shape
    blocks = lax.axis_size("seq")
    copies = lax.axis_size("chan")
    group = width // blocks
    rank = lax.axis_index("chan")
    limit = pltpu.CompilerParams(vmem_limit_bytes=48 * 1024 * 1024)
    packed = jax.ShapeDtypeStruct((blocks, 3 * group, rows), BF16)
    sent = pl.pallas_call(
        pack_kernel, out_shape=packed, in_specs=[VMEM] * 4, out_specs=VMEM, compiler_params=limit
    )(values, gates, grad_out, filter_raw)
    held = lax.all_to_all(sent, "seq", split_axis=0, concat_axis=0, tiled=True)
    consts = tables(blocks, rows)
    done = pl.pallas_call(
        spectra_kernel,
        out_shape=packed,
        in_specs=[VMEM] * (1 + len(consts)),
        out_specs=VMEM,
        scratch_shapes=[
            pltpu.VMEM((3, blocks * group, rows), F32),
            pltpu.VMEM((3, blocks * group, rows), F32),
        ],
        compiler_params=limit,
    )(held, *consts)
    back = lax.all_to_all(done, "seq", split_axis=0, concat_axis=0, tiled=True)
    terms = back[:, 2 * group :, :]
    share = blocks // copies
    pieces = [
        lax.dynamic_slice_in_dim(terms, lax.rem(rank + d, copies) * share, share, 0)
        for d in range(copies)
    ]
    for d in range(1, copies):
        pieces[d] = lax.ppermute(
            pieces[d], "chan", [(src, (src + d) % copies) for src in range(copies)]
        )
    shape = jax.ShapeDtypeStruct((rows, width), BF16)
    value_grad, gate_grad = pl.pallas_call(
        finish_kernel,
        out_shape=(shape, shape),
        in_specs=[VMEM] * 5,
        out_specs=(VMEM, VMEM),
        compiler_params=limit,
    )(values, gates, grad_out, skip_gain[None, :], back)
    filter_grad = pl.pallas_call(
        sum_kernel,
        out_shape=jax.ShapeDtypeStruct((rows, width // copies), F32),
        in_specs=[VMEM] * copies,
        out_specs=VMEM,
        compiler_params=limit,
    )(*pieces)
    return (value_grad, gate_grad, filter_grad)


def solution(mesh):
    in_specs = (P("seq", "chan"), P("seq", "chan"), P("seq", "chan"), P("seq", None), P("chan"))
    out_specs = (P("seq", "chan"), P("seq", "chan"), P("seq", "chan"))
    return jax.shard_map(local, mesh=mesh, in_specs=in_specs, out_specs=out_specs, check_vma=False)
```

```python
import math

import jax
import jax.numpy as jnp
import numpy as np
from jax import lax
from jax.experimental import pallas as pl
from jax.experimental.pallas import tpu as pltpu
from jax.sharding import PartitionSpec as P

F32 = jnp.float32
BF16 = jnp.bfloat16
VMEM = pl.BlockSpec(memory_space=pltpu.VMEM)
SHARES = 4
GROUP = 16
STEP = GROUP // SHARES
TAIL = 8
WIDE = True


def split_pair(table):
    high = table.astype(np.float32).astype(jnp.bfloat16)
    low = (table - high.astype(np.float64)).astype(np.float32).astype(jnp.bfloat16)
    return high, low


def tables(blocks, rows):
    period = 2 * blocks * rows
    scale = 2.0 / period / math.sqrt(blocks * rows)
    half = np.arange(blocks) + 0.5
    block_angle = 2.0 * np.pi / (2 * blocks) * np.outer(half, np.arange(blocks))
    enter = np.concatenate([np.cos(block_angle), -np.sin(block_angle)], axis=0)
    leave = np.concatenate([np.cos(block_angle), -np.sin(block_angle)], axis=0).T * scale
    turn = 2.0 * np.pi / period * np.outer(half, np.arange(rows))
    row_angle = 2.0 * np.pi / rows * np.outer(np.arange(rows), np.arange(rows))
    row_cos, row_sin = np.cos(row_angle), np.sin(row_angle)
    forward = np.block([[row_cos, -row_sin], [row_sin, row_cos]])
    inverse = np.block([[row_cos, row_sin], [-row_sin, row_cos]])
    enter_pair = np.concatenate(split_pair(enter), axis=0)
    leave_high, leave_low = split_pair(leave)
    leave_pair = np.concatenate([leave_high, leave_low], axis=0)
    if not WIDE:
        enter_pair = enter_pair[: 2 * blocks]
    return (
        enter_pair,
        leave_pair,
        *split_pair(forward),
        *split_pair(inverse),
        np.cos(turn).astype(np.float32),
        np.sin(turn).astype(np.float32),
    )


def split_value(x):
    high = x.astype(BF16)
    return high, (x - high.astype(F32)).astype(BF16)


def dot(a, b):
    return jnp.dot(a, b, preferred_element_type=F32)


def dot_wide(x, high, low):
    if not WIDE:
        return dot(x.astype(BF16), high)
    x_high, x_low = split_value(x)
    return dot(x_high, high) + (dot(x_low, high) + dot(x_high, low))


def pack_kernel(values_ref, gates_ref, grad_ref, filter_ref, out_ref, values, gates, grad, taps, flat, mixed, sems):
    group = out_ref.shape[1] // 3
    blocks = out_ref.shape[0]
    share = group // SHARES
    copies = [
        pltpu.make_async_copy(src, dst, sems.at[k])
        for k, (src, dst) in enumerate(
            ((values_ref, values), (filter_ref, taps), (gates_ref, gates), (grad_ref, grad))
        )
    ]
    for copy in copies:
        copy.start()

    def place(a, part):
        flat[a] = part.T
        for q in range(SHARES):
            for i in range(share):
                row = flat[a, pl.ds(q * share * blocks + i, blocks, stride=share), :]
                mixed[a, pl.ds(q * share + i, blocks, stride=group), :] = row
        turned = mixed[a].astype(BF16)
        out_ref[:, a * group : (a + 1) * group, :] = turned.reshape(blocks, group, -1)

    copies[0].wait()
    place(0, values[...].astype(F32))
    copies[1].wait()
    place(2, taps[...].astype(F32))
    copies[2].wait()
    copies[3].wait()
    place(1, (grad[...] * gates[...].astype(F32)).astype(BF16).astype(F32))


def spectrum(wide, a, c0, enter_ref, fwd_h, fwd_l, cos_t, sin_t):
    blocks, rows = cos_t.shape
    cols = [wide[a, pl.ds(c0 + c, blocks, stride=GROUP), :] for c in range(STEP)]
    mixed = dot(enter_ref[...], jnp.concatenate(cols, axis=1).astype(BF16))
    if enter_ref.shape[0] > 2 * blocks:
        mixed = mixed[: 2 * blocks] + mixed[2 * blocks :]
    turned = []
    for c in range(STEP):
        re = mixed[:blocks, c * rows : (c + 1) * rows]
        im = mixed[blocks:, c * rows : (c + 1) * rows]
        turned.append(jnp.concatenate([re * cos_t + im * sin_t, im * cos_t - re * sin_t], axis=1))
    return dot_wide(jnp.concatenate(turned, axis=0), fwd_h[...], fwd_l[...])


def signal(re, im, leave_ref, inv_h, inv_l, cos_t, sin_t):
    blocks, rows = cos_t.shape
    full = dot_wide(jnp.concatenate([re, im], axis=1), inv_h[...], inv_l[...])
    cols = []
    for c in range(STEP):
        re = full[c * blocks : (c + 1) * blocks, :rows]
        im = full[c * blocks : (c + 1) * blocks, rows:]
        cols.append(jnp.concatenate([re * cos_t - im * sin_t, re * sin_t + im * cos_t], axis=0))
    joined = jnp.concatenate(cols, axis=1)
    if not WIDE:
        return dot(leave_ref[:blocks, :], joined.astype(BF16))
    high, low = split_value(joined)
    pair = dot(leave_ref[...], high)
    return pair[:blocks] + (pair[blocks:] + dot(leave_ref[:blocks, :], low))


def conj_product(left, right):
    rows = left.shape[1] // 2
    l_re, l_im, r_re, r_im = left[:, :rows], left[:, rows:], right[:, :rows], right[:, rows:]
    return l_re * r_re + l_im * r_im, l_re * r_im - l_im * r_re


def plain_product(left, right):
    rows = left.shape[1] // 2
    l_re, l_im, r_re, r_im = left[:, :rows], left[:, rows:], right[:, :rows], right[:, rows:]
    return l_re * r_re - l_im * r_im, l_re * r_im + l_im * r_re


def chunk(ref, c0, blocks):
    return ref[pl.ds(c0 * blocks, STEP * blocks), :]


def terms_kernel(
    rank_ref, in_ref, enter_ref, leave_ref, fwd_h, fwd_l, inv_h, inv_l, cos_ref, sin_ref, *rest
):
    pieces, (v_ref, g_ref, wide) = rest[:SHARES], rest[SHARES:]
    blocks, rows = in_ref.shape[0], in_ref.shape[2]
    cos_t, sin_t = cos_ref[...], sin_ref[...]
    for a in range(2):
        part = in_ref[:, a * GROUP : (a + 1) * GROUP, :]
        wide[a] = part.astype(F32).reshape(blocks * GROUP, rows)
    for c0 in range(0, GROUP, STEP):
        for a, ref in enumerate((v_ref, g_ref)):
            ref[c0 * blocks : (c0 + STEP) * blocks, :] = spectrum(
                wide, a, c0, enter_ref, fwd_h, fwd_l, cos_t, sin_t
            )
    rank = rank_ref[0]
    for d in range(SHARES):
        start = pl.multiple_of(lax.rem(rank + d, SHARES) * (STEP * blocks), STEP * blocks)
        v = v_ref[pl.ds(start, STEP * blocks), :]
        g = g_ref[pl.ds(start, STEP * blocks), :]
        out = signal(*conj_product(v, g), leave_ref, inv_h, inv_l, cos_t, sin_t)
        for c in range(STEP):
            pieces[d][c] = out[:, c * rows : (c + 1) * rows].astype(BF16)


def conv_kernel(
    in_ref, v_ref, enter_ref, leave_ref, fwd_h, fwd_l, inv_h, inv_l, cos_ref, sin_ref, out_ref, h_ref, wide, result
):
    blocks, rows = in_ref.shape[0], in_ref.shape[2]
    cos_t, sin_t = cos_ref[...], sin_ref[...]
    wide[0] = in_ref[:, 2 * GROUP :, :].astype(F32).reshape(blocks * GROUP, rows)
    for c0 in range(0, GROUP, STEP):
        h = spectrum(wide, 0, c0, enter_ref, fwd_h, fwd_l, cos_t, sin_t)
        h_ref[c0 * blocks : (c0 + STEP) * blocks, :] = h
        out = signal(*plain_product(h, chunk(v_ref, c0, blocks)), leave_ref, inv_h, inv_l, cos_t, sin_t)
        for c in range(STEP):
            result[pl.ds(c0 + c, blocks, stride=GROUP), :] = out[:, c * rows : (c + 1) * rows]
    out_ref[...] = result[...].astype(BF16).reshape(blocks, GROUP, rows)


def back_kernel(
    conv_ref, h_ref, g_ref, leave_ref, inv_h, inv_l, cos_ref, sin_ref, *rest
):
    pieces, (out_ref, result, tail) = rest[:SHARES], rest[SHARES:]
    blocks, rows = conv_ref.shape[0], conv_ref.shape[2]
    cos_t, sin_t = cos_ref[...], sin_ref[...]
    for c0 in range(0, GROUP, STEP):
        out = signal(
            *conj_product(chunk(h_ref, c0, blocks), chunk(g_ref, c0, blocks)),
            leave_ref, inv_h, inv_l, cos_t, sin_t,
        )
        for c in range(STEP):
            result[pl.ds(c0 + c, blocks, stride=GROUP), :] = out[:, c * rows : (c + 1) * rows]
    out_ref[:, :GROUP, :] = conv_ref[...]
    out_ref[:, GROUP : 2 * GROUP, :] = result[...].astype(BF16).reshape(blocks, GROUP, rows)
    tail[...] = jnp.zeros_like(tail)
    for c in range(STEP):
        total = pieces[0][c].astype(F32)
        for piece in pieces[1:]:
            total = total + piece[c].astype(F32)
        tail[pl.ds(c, blocks, stride=TAIL), :] = total
    out_ref[:, 2 * GROUP :, :] = tail[...].astype(BF16).reshape(blocks, TAIL, rows)


def finish_kernel(values_ref, gates_ref, grad_ref, skip_ref, in_ref, value_out, gate_out, filter_out, flat, mixed):
    blocks, rows = in_ref.shape[0], in_ref.shape[2]
    share = GROUP // SHARES

    def part(a):
        mixed[a] = in_ref[:, a * GROUP : (a + 1) * GROUP, :].astype(F32).reshape(-1, rows)
        for q in range(SHARES):
            for i in range(share):
                row = mixed[a, pl.ds(q * share + i, blocks, stride=GROUP), :]
                flat[a, pl.ds(q * share * blocks + i, blocks, stride=share), :] = row
        return flat[a].T

    grad = grad_ref[...]
    skip = skip_ref[...]
    gate_out[...] = (grad * (part(0) + skip * values_ref[...].astype(F32))).astype(BF16)
    gate_term = (grad * gates_ref[...].astype(F32)).astype(BF16).astype(F32)
    value_out[...] = (part(1) + skip * gate_term).astype(BF16)
    tail = in_ref[:, 2 * GROUP :, :].astype(F32).reshape(-1, rows)
    mixed[0, : blocks * TAIL, :] = tail
    for i in range(share):
        row = mixed[0, pl.ds(i, blocks, stride=TAIL), :]
        flat[0, pl.ds(i, blocks, stride=share), :] = row
    filter_out[...] = flat[0, : blocks * share, :].T


def call(kernel, out_shape, args, scratch, specs=None):
    outs = jax.tree.map(lambda _: VMEM, out_shape)
    return pl.pallas_call(
        kernel,
        out_shape=out_shape,
        in_specs=specs or [VMEM] * len(args),
        out_specs=outs,
        scratch_shapes=scratch,
        compiler_params=pltpu.CompilerParams(vmem_limit_bytes=48 * 1024 * 1024),
    )(*args)


def transforms(held, rank, consts, exchange):
    blocks, _, rows = held.shape
    enter, leave, fwd_h, fwd_l, inv_h, inv_l, cos_t, sin_t = consts
    piece = jax.ShapeDtypeStruct((STEP, blocks, rows), BF16)
    spec = jax.ShapeDtypeStruct((GROUP * blocks, 2 * rows), F32)
    wide = pltpu.VMEM((GROUP * blocks, rows), F32)
    *pieces, v, g = call(
        terms_kernel,
        (piece,) * SHARES + (spec, spec),
        (rank, held, *consts),
        [pltpu.VMEM((2, GROUP * blocks, rows), F32)],
        [pl.BlockSpec(memory_space=pltpu.SMEM)] + [VMEM] * 9,
    )
    pieces = exchange(pieces)
    conv, h = call(
        conv_kernel,
        (jax.ShapeDtypeStruct((blocks, GROUP, rows), BF16), spec),
        (held, v, *consts),
        [pltpu.VMEM((1, GROUP * blocks, rows), F32), wide],
    )
    return call(
        back_kernel,
        jax.ShapeDtypeStruct((blocks, 2 * GROUP + TAIL, rows), BF16),
        (conv, h, g, leave, inv_h, inv_l, cos_t, sin_t, *pieces),
        [wide, pltpu.VMEM((TAIL * blocks, rows), F32)],
    )


def local(values, gates, grad_out, filter_raw, skip_gain):
    rows, width = values.shape
    blocks = lax.axis_size("seq")
    rank = lax.axis_index("chan").astype(jnp.int32).reshape(1)
    flat = pltpu.VMEM((3, width, rows), F32)
    sent = call(
        pack_kernel,
        jax.ShapeDtypeStruct((blocks, 3 * GROUP, rows), BF16),
        (values, gates, grad_out, filter_raw),
        [
            pltpu.VMEM((rows, width), BF16),
            pltpu.VMEM((rows, width), BF16),
            pltpu.VMEM((rows, width), F32),
            pltpu.VMEM((rows, width), BF16),
            flat,
            flat,
            pltpu.SemaphoreType.DMA((4,)),
        ],
        [pl.BlockSpec(memory_space=pl.ANY)] * 4,
    )
    held = lax.all_to_all(sent, "seq", split_axis=0, concat_axis=0, tiled=True)

    def exchange(pieces):
        return [pieces[0]] + [
            lax.ppermute(pieces[d], "chan", [(src, (src + d) % SHARES) for src in range(SHARES)])
            for d in range(1, SHARES)
        ]

    done = transforms(held, rank, tables(blocks, rows), exchange)
    back = lax.all_to_all(done, "seq", split_axis=0, concat_axis=0, tiled=True)
    shape = jax.ShapeDtypeStruct((rows, width), BF16)
    pair = pltpu.VMEM((2, width, rows), F32)
    return call(
        finish_kernel,
        (shape, shape, jax.ShapeDtypeStruct((rows, width // SHARES), F32)),
        (values, gates, grad_out, skip_gain[None, :], back),
        [pair, pair],
    )


def solution(mesh):
    in_specs = (P("seq", "chan"), P("seq", "chan"), P("seq", "chan"), P("seq", None), P("chan"))
    out_specs = (P("seq", "chan"), P("seq", "chan"), P("seq", "chan"))
    return jax.shard_map(local, mesh=mesh, in_specs=in_specs, out_specs=out_specs, check_vma=False)
```

```python
import math

import jax
import jax.numpy as jnp
import numpy as np
from jax import lax
from jax.experimental import pallas as pl
from jax.experimental.pallas import tpu as pltpu
from jax.sharding import PartitionSpec as P

F32 = jnp.float32
BF16 = jnp.bfloat16
VMEM = pl.BlockSpec(memory_space=pltpu.VMEM)
SHARE = 4
SENT = 10
BACK = 12
WIDE = True


def split_pair(table):
    high = table.astype(np.float32).astype(jnp.bfloat16)
    low = (table - high.astype(np.float64)).astype(np.float32).astype(jnp.bfloat16)
    return high, low


def tables(blocks, rows):
    period = 2 * blocks * rows
    scale = 2.0 / period / math.sqrt(blocks * rows)
    half = np.arange(blocks) + 0.5
    block_angle = 2.0 * np.pi / (2 * blocks) * np.outer(half, np.arange(blocks))
    enter = np.concatenate([np.cos(block_angle), -np.sin(block_angle)], axis=0)
    leave = np.concatenate([np.cos(block_angle), -np.sin(block_angle)], axis=0).T * scale
    turn = 2.0 * np.pi / period * np.outer(half, np.arange(rows))
    row_angle = 2.0 * np.pi / rows * np.outer(np.arange(rows), np.arange(rows))
    row_cos, row_sin = np.cos(row_angle), np.sin(row_angle)
    forward = np.block([[row_cos, -row_sin], [row_sin, row_cos]])
    inverse = np.block([[row_cos, row_sin], [-row_sin, row_cos]])
    enter_pair = np.concatenate(split_pair(enter), axis=0)
    leave_high, leave_low = split_pair(leave)
    leave_pair = np.concatenate([leave_high, leave_low], axis=0)
    if not WIDE:
        enter_pair, leave_pair = enter_pair[: 2 * blocks], leave_pair[:blocks]
    return (
        enter_pair,
        leave_pair,
        *split_pair(forward),
        *split_pair(inverse),
        np.cos(turn).astype(np.float32),
        np.sin(turn).astype(np.float32),
    )


def split_value(x):
    high = x.astype(BF16)
    return high, (x - high.astype(F32)).astype(BF16)


def dot(a, b):
    return jnp.dot(a, b, preferred_element_type=F32)


def dot_wide(x, high, low):
    if not WIDE:
        return dot(x.astype(BF16), high)
    x_high, x_low = split_value(x)
    return dot(x_high, high) + (dot(x_low, high) + dot(x_high, low))


def pack_kernel(rank_ref, values_ref, gates_ref, grad_ref, filter_ref, out_ref, values, gates, grad, taps, flat, rows_ref, sems):
    pairs = flat.shape[0] // SHARE
    copies = [
        pltpu.make_async_copy(src, dst, sems.at[k])
        for k, (src, dst) in enumerate(
            ((values_ref, values), (filter_ref, taps), (gates_ref, gates), (grad_ref, grad))
        )
    ]
    for copy in copies:
        copy.start()

    def place(part, sources, start):
        flat[...] = part.T
        for k, source in enumerate(sources):
            rows_ref[pl.ds(start + k, pairs, stride=SENT), :] = flat[
                pl.ds(source, pairs, stride=SHARE), :
            ]

    copies[0].wait()
    place(values[...].astype(F32), range(SHARE), 0)
    copies[1].wait()
    place(taps[...].astype(F32), (rank_ref[0], rank_ref[0]), 2 * SHARE)
    copies[2].wait()
    copies[3].wait()
    gate_term = (grad[...] * gates[...].astype(F32)).astype(BF16).astype(F32)
    place(gate_term, range(SHARE), SHARE)
    out_ref[...] = rows_ref[...].astype(BF16)


def spectra_kernel(
    in_ref, enter_ref, leave_ref, fwd_h, fwd_l, inv_h, inv_l, cos_ref, sin_ref, out_ref, wide, result
):
    blocks, rows = cos_ref.shape
    copies = in_ref.shape[0] // (blocks * SENT)
    cos_t, sin_t = cos_ref[...], sin_ref[...]
    wide[...] = in_ref[...].astype(F32)

    def spectrum(starts):
        cols = [wide[pl.ds(start, blocks, stride=SENT), :] for start in starts]
        mixed = dot(enter_ref[...], jnp.concatenate(cols, axis=1).astype(BF16))
        if WIDE:
            mixed = mixed[: 2 * blocks] + mixed[2 * blocks :]
        turned = []
        for c in range(SHARE):
            re = mixed[:blocks, c * rows : (c + 1) * rows]
            im = mixed[blocks:, c * rows : (c + 1) * rows]
            turned.append(
                jnp.concatenate([re * cos_t + im * sin_t, im * cos_t - re * sin_t], axis=1)
            )
        full = dot_wide(jnp.concatenate(turned, axis=0), fwd_h[...], fwd_l[...])
        return full[:, :rows], full[:, rows:]

    def signal(re, im):
        full = dot_wide(jnp.concatenate([re, im], axis=1), inv_h[...], inv_l[...])
        cols = []
        for c in range(SHARE):
            re = full[c * blocks : (c + 1) * blocks, :rows]
            im = full[c * blocks : (c + 1) * blocks, rows:]
            cols.append(
                jnp.concatenate([re * cos_t - im * sin_t, re * sin_t + im * cos_t], axis=0)
            )
        joined = jnp.concatenate(cols, axis=1)
        if not WIDE:
            mixed = dot(leave_ref[...], joined.astype(BF16))
        else:
            high, low = split_value(joined)
            pair = dot(leave_ref[...], high)
            mixed = pair[:blocks] + (pair[blocks:] + dot(leave_ref[:blocks, :], low))
        return [mixed[:, c * rows : (c + 1) * rows] for c in range(SHARE)]

    def put(block, first, cols):
        for c, col in enumerate(cols):
            result[pl.ds(block * blocks * BACK + first + c, blocks, stride=BACK), :] = col

    h_re, h_im = spectrum([c * blocks * SENT + 2 * SHARE for c in range(SHARE)])
    f_re = f_im = None
    for j in range(copies):
        base = j * blocks * SENT
        v_re, v_im = spectrum([base + c for c in range(SHARE)])
        put(j, 0, signal(h_re * v_re - h_im * v_im, h_re * v_im + h_im * v_re))
        g_re, g_im = spectrum([base + SHARE + c for c in range(SHARE)])
        put(j, SHARE, signal(h_re * g_re + h_im * g_im, h_re * g_im - h_im * g_re))
        re, im = v_re * g_re + v_im * g_im, v_re * g_im - v_im * g_re
        f_re, f_im = (re, im) if j == 0 else (f_re + re, f_im + im)
    terms = signal(f_re, f_im)
    for j in range(copies):
        put(j, 2 * SHARE, terms)
    out_ref[...] = result[...].astype(BF16)


def finish_kernel(
    rank_ref, values_ref, gates_ref, grad_ref, skip_ref, in_ref, value_out, gate_out, filter_out, wide, flat
):
    pairs = flat.shape[0] // SHARE
    own = filter_out.shape[1]
    wide[...] = in_ref[...].astype(F32)

    def part(first):
        for c in range(SHARE):
            flat[pl.ds(c, pairs, stride=SHARE), :] = wide[pl.ds(first + c, pairs, stride=BACK), :]
        return flat[...].T

    grad = grad_ref[...]
    skip = skip_ref[...]
    gate_out[...] = (grad * (part(0) + skip * values_ref[...].astype(F32))).astype(BF16)
    gate_term = (grad * gates_ref[...].astype(F32)).astype(BF16).astype(F32)
    value_out[...] = (part(SHARE) + skip * gate_term).astype(BF16)
    start = rank_ref[0] * (own // SHARE * BACK) + 2 * SHARE
    for c in range(SHARE):
        flat[pl.ds(c, own // SHARE, stride=SHARE), :] = wide[
            pl.ds(start + c, own // SHARE, stride=BACK), :
        ]
    filter_out[...] = flat[:own, :].T


def call(kernel, out_shape, args, scratch, specs=None, limit=48):
    return pl.pallas_call(
        kernel,
        out_shape=out_shape,
        in_specs=specs or [VMEM] * len(args),
        out_specs=jax.tree.map(lambda _: VMEM, out_shape),
        scratch_shapes=scratch,
        compiler_params=pltpu.CompilerParams(vmem_limit_bytes=limit * 1024 * 1024),
    )(*args)


def exchange(x):
    shaped = x.reshape(lax.axis_size("chan") * lax.axis_size("seq"), -1, 2, x.shape[1])
    moved = lax.all_to_all(shaped, ("chan", "seq"), split_axis=0, concat_axis=0, tiled=True)
    return moved.reshape(x.shape)


def transform(held, blocks):
    rows = held.shape[1]
    back = held.shape[0] // SENT * BACK
    consts = tables(blocks, rows)
    return call(
        spectra_kernel,
        jax.ShapeDtypeStruct((back, rows), BF16),
        (held, *consts),
        [pltpu.VMEM(held.shape, F32), pltpu.VMEM((back, rows), F32)],
    )


def local(values, gates, grad_out, filter_raw, skip_gain):
    rows, width = values.shape
    blocks = lax.axis_size("seq")
    pairs = blocks * lax.axis_size("chan")
    rank = lax.axis_index("chan").astype(jnp.int32).reshape(1)
    flat = pltpu.VMEM((width, rows), F32)
    scalar = pl.BlockSpec(memory_space=pltpu.SMEM)
    sent = call(
        pack_kernel,
        jax.ShapeDtypeStruct((pairs * SENT, rows), BF16),
        (rank, values, gates, grad_out, filter_raw),
        [
            pltpu.VMEM((rows, width), BF16),
            pltpu.VMEM((rows, width), BF16),
            pltpu.VMEM((rows, width), F32),
            pltpu.VMEM((rows, width), BF16),
            flat,
            pltpu.VMEM((pairs * SENT, rows), F32),
            pltpu.SemaphoreType.DMA((4,)),
        ],
        [scalar] + [pl.BlockSpec(memory_space=pltpu.HBM)] * 4,
        limit=60,
    )
    back = exchange(transform(exchange(sent), blocks))
    shape = jax.ShapeDtypeStruct((rows, width), BF16)
    return call(
        finish_kernel,
        (shape, shape, jax.ShapeDtypeStruct((rows, width // lax.axis_size("chan")), F32)),
        (rank, values, gates, grad_out, skip_gain[None, :], back),
        [pltpu.VMEM(back.shape, F32), flat],
        [scalar] + [VMEM] * 5,
    )


def solution(mesh):
    in_specs = (P("seq", "chan"), P("seq", "chan"), P("seq", "chan"), P("seq", None), P("chan"))
    out_specs = (P("seq", "chan"), P("seq", "chan"), P("seq", "chan"))
    return jax.shard_map(local, mesh=mesh, in_specs=in_specs, out_specs=out_specs, check_vma=False)
```

```python
import math

import jax
import jax.numpy as jnp
import numpy as np
from jax import lax
from jax.experimental import pallas as pl
from jax.experimental.pallas import tpu as pltpu
from jax.sharding import PartitionSpec as P

F32 = jnp.float32
BF16 = jnp.bfloat16
VMEM = pl.BlockSpec(memory_space=pltpu.VMEM)
SHARE = 4
LINES = 10
WIDE = True


def split_pair(table):
    high = table.astype(np.float32).astype(jnp.bfloat16)
    low = (table - high.astype(np.float64)).astype(np.float32).astype(jnp.bfloat16)
    return high, low


def tables(blocks, rows):
    period = 2 * blocks * rows
    scale = 2.0 / period / math.sqrt(blocks * rows)
    half = np.arange(blocks) + 0.5
    block_angle = 2.0 * np.pi / (2 * blocks) * np.outer(half, np.arange(blocks))
    enter = np.concatenate([np.cos(block_angle), -np.sin(block_angle)], axis=0)
    leave = np.concatenate([np.cos(block_angle), -np.sin(block_angle)], axis=0).T * scale
    turn = 2.0 * np.pi / period * np.outer(half, np.arange(rows))
    row_angle = 2.0 * np.pi / rows * np.outer(np.arange(rows), np.arange(rows))
    row_cos, row_sin = np.cos(row_angle), np.sin(row_angle)
    forward = np.block([[row_cos, -row_sin], [row_sin, row_cos]])
    inverse = np.block([[row_cos, row_sin], [-row_sin, row_cos]])
    enter_pair = np.concatenate(split_pair(enter), axis=0)
    leave_high, leave_low = split_pair(leave)
    leave_pair = np.concatenate([leave_high, leave_low], axis=0)
    if not WIDE:
        enter_pair, leave_pair = enter_pair[: 2 * blocks], leave_pair[:blocks]
    return (
        enter_pair,
        leave_pair,
        *split_pair(forward),
        *split_pair(inverse),
        np.cos(turn).astype(np.float32),
        np.sin(turn).astype(np.float32),
    )


def split_value(x):
    high = x.astype(BF16)
    return high, (x - high.astype(F32)).astype(BF16)


def dot(a, b):
    return jnp.dot(a, b, preferred_element_type=F32)


def dot_wide(x, high, low):
    if not WIDE:
        return dot(x.astype(BF16), high)
    x_high, x_low = split_value(x)
    return dot(x_high, high) + (dot(x_low, high) + dot(x_high, low))


def pack_kernel(rank_ref, values_ref, gates_ref, grad_ref, filter_ref, out_ref, values, gates, grad, taps, rows_ref, sems):
    pairs = rows_ref.shape[0] // LINES
    copies = [
        pltpu.make_async_copy(src, dst, sems.at[k])
        for k, (src, dst) in enumerate(
            ((values_ref, values), (filter_ref, taps), (gates_ref, gates), (grad_ref, grad))
        )
    ]
    for copy in copies:
        copy.start()

    def put(line, rows):
        rows_ref[pl.ds(line, pairs, stride=LINES), :] = rows

    def place(part, first):
        turned = part.T
        for q in range(SHARE):
            put(first + q, turned[q * pairs : (q + 1) * pairs, :])

    copies[0].wait()
    place(values[...].astype(F32), 0)
    copies[1].wait()
    start = pl.multiple_of(rank_ref[0] * pairs, pairs)
    own = taps[:, pl.ds(start, pairs)].astype(F32).T
    for line in range(2 * SHARE, LINES):
        put(line, own)
    copies[2].wait()
    copies[3].wait()
    gate_term = (grad[...] * gates[...].astype(F32)).astype(BF16).astype(F32)
    place(gate_term, SHARE)
    out_ref[...] = rows_ref[...].astype(BF16)


def spectra_kernel(
    in_ref, enter_ref, leave_ref, fwd_h, fwd_l, inv_h, inv_l, cos_ref, sin_ref, out_ref, wide, result
):
    blocks, rows = cos_ref.shape
    copies = in_ref.shape[0] // (blocks * LINES)
    cos_t, sin_t = cos_ref[...], sin_ref[...]
    wide[...] = in_ref[...].astype(F32)

    def spectrum(starts):
        cols = [wide[pl.ds(start, blocks, stride=LINES), :] for start in starts]
        mixed = dot(enter_ref[...], jnp.concatenate(cols, axis=1).astype(BF16))
        if WIDE:
            mixed = mixed[: 2 * blocks] + mixed[2 * blocks :]
        turned = []
        for c in range(SHARE):
            re = mixed[:blocks, c * rows : (c + 1) * rows]
            im = mixed[blocks:, c * rows : (c + 1) * rows]
            turned.append(
                jnp.concatenate([re * cos_t + im * sin_t, im * cos_t - re * sin_t], axis=1)
            )
        full = dot_wide(jnp.concatenate(turned, axis=0), fwd_h[...], fwd_l[...])
        return full[:, :rows], full[:, rows:]

    def signal(re, im):
        full = dot_wide(jnp.concatenate([re, im], axis=1), inv_h[...], inv_l[...])
        cols = []
        for c in range(SHARE):
            re = full[c * blocks : (c + 1) * blocks, :rows]
            im = full[c * blocks : (c + 1) * blocks, rows:]
            cols.append(
                jnp.concatenate([re * cos_t - im * sin_t, re * sin_t + im * cos_t], axis=0)
            )
        joined = jnp.concatenate(cols, axis=1)
        if not WIDE:
            mixed = dot(leave_ref[...], joined.astype(BF16))
        else:
            high, low = split_value(joined)
            pair = dot(leave_ref[...], high)
            mixed = pair[:blocks] + (pair[blocks:] + dot(leave_ref[:blocks, :], low))
        return [mixed[:, c * rows : (c + 1) * rows] for c in range(SHARE)]

    def put(block, first, cols):
        for c, col in enumerate(cols):
            result[pl.ds(block * blocks * LINES + first + c, blocks, stride=LINES), :] = col

    h_re, h_im = spectrum([c * blocks * LINES + 2 * SHARE for c in range(SHARE)])
    f_re = f_im = None
    for j in range(copies):
        base = j * blocks * LINES
        v_re, v_im = spectrum([base + c for c in range(SHARE)])
        put(j, 0, signal(h_re * v_re - h_im * v_im, h_re * v_im + h_im * v_re))
        g_re, g_im = spectrum([base + SHARE + c for c in range(SHARE)])
        put(j, SHARE, signal(h_re * g_re + h_im * g_im, h_re * g_im - h_im * g_re))
        re, im = v_re * g_re + v_im * g_im, v_re * g_im - v_im * g_re
        f_re, f_im = (re, im) if j == 0 else (f_re + re, f_im + im)
    terms = signal(f_re, f_im)
    for j in range(copies):
        for line in range(2 * SHARE, LINES):
            put(j, line, [terms[j]])
    out_ref[...] = result[...].astype(BF16)


def finish_kernel(
    values_ref, gates_ref, grad_ref, skip_ref, in_ref, value_out, gate_out, filter_out, wide, flat
):
    pairs = flat.shape[0] // SHARE
    wide[...] = in_ref[...].astype(F32)

    def part(first):
        for q in range(SHARE):
            flat[q * pairs : (q + 1) * pairs, :] = wide[
                pl.ds(first + q, pairs, stride=LINES), :
            ]
        return flat[...].T

    grad = grad_ref[...]
    skip = skip_ref[...]
    gate_out[...] = (grad * (part(0) + skip * values_ref[...].astype(F32))).astype(BF16)
    gate_term = (grad * gates_ref[...].astype(F32)).astype(BF16).astype(F32)
    value_out[...] = (part(SHARE) + skip * gate_term).astype(BF16)
    filter_out[...] = wide[pl.ds(2 * SHARE, pairs, stride=LINES), :].T


def call(kernel, out_shape, args, scratch, specs=None, limit=48):
    return pl.pallas_call(
        kernel,
        out_shape=out_shape,
        in_specs=specs or [VMEM] * len(args),
        out_specs=jax.tree.map(lambda _: VMEM, out_shape),
        scratch_shapes=scratch,
        compiler_params=pltpu.CompilerParams(vmem_limit_bytes=limit * 1024 * 1024),
    )(*args)


def exchange(x):
    shaped = x.reshape(lax.axis_size("chan") * lax.axis_size("seq"), -1, 2, x.shape[1])
    moved = lax.all_to_all(shaped, ("chan", "seq"), split_axis=0, concat_axis=0, tiled=True)
    return moved.reshape(x.shape)


def transform(held, blocks):
    rows = held.shape[1]
    consts = tables(blocks, rows)
    return call(
        spectra_kernel,
        jax.ShapeDtypeStruct(held.shape, BF16),
        (held, *consts),
        [pltpu.VMEM(held.shape, F32), pltpu.VMEM(held.shape, F32)],
    )


def local(values, gates, grad_out, filter_raw, skip_gain):
    rows, width = values.shape
    blocks = lax.axis_size("seq")
    pairs = blocks * lax.axis_size("chan")
    rank = lax.axis_index("chan").astype(jnp.int32).reshape(1)
    flat = pltpu.VMEM((width, rows), F32)
    scalar = pl.BlockSpec(memory_space=pltpu.SMEM)
    sent = call(
        pack_kernel,
        jax.ShapeDtypeStruct((pairs * LINES, rows), BF16),
        (rank, values, gates, grad_out, filter_raw),
        [
            pltpu.VMEM((rows, width), BF16),
            pltpu.VMEM((rows, width), BF16),
            pltpu.VMEM((rows, width), F32),
            pltpu.VMEM((rows, width), BF16),
            pltpu.VMEM((pairs * LINES, rows), F32),
            pltpu.SemaphoreType.DMA((4,)),
        ],
        [scalar] + [pl.BlockSpec(memory_space=pltpu.HBM)] * 4,
        limit=60,
    )
    back = exchange(transform(exchange(sent), blocks))
    shape = jax.ShapeDtypeStruct((rows, width), BF16)
    return call(
        finish_kernel,
        (shape, shape, jax.ShapeDtypeStruct((rows, width // lax.axis_size("chan")), F32)),
        (values, gates, grad_out, skip_gain[None, :], back),
        [pltpu.VMEM(back.shape, F32), flat],
    )


def solution(mesh):
    in_specs = (P("seq", "chan"), P("seq", "chan"), P("seq", "chan"), P("seq", None), P("chan"))
    out_specs = (P("seq", "chan"), P("seq", "chan"), P("seq", "chan"))
    return jax.shard_map(local, mesh=mesh, in_specs=in_specs, out_specs=out_specs, check_vma=False)
```

```python
import math

import jax
import jax.numpy as jnp
import numpy as np
from jax import lax
from jax.experimental import pallas as pl
from jax.experimental.pallas import tpu as pltpu
from jax.sharding import PartitionSpec as P

F32 = jnp.float32
BF16 = jnp.bfloat16
VMEM = pl.BlockSpec(memory_space=pltpu.VMEM)
SHARE = 4
PIECES = 4
LINES = 10


def split_pair(table):
    high = table.astype(np.float32).astype(jnp.bfloat16)
    low = (table - high.astype(np.float64)).astype(np.float32).astype(jnp.bfloat16)
    return high, low


def tables(blocks, rows):
    period = 2 * blocks * rows
    scale = 2.0 / period / math.sqrt(blocks * rows)
    half = np.arange(blocks) + 0.5
    block_angle = 2.0 * np.pi / (2 * blocks) * np.outer(half, np.arange(blocks))
    enter = np.concatenate([np.cos(block_angle), -np.sin(block_angle)], axis=0)
    leave = np.concatenate([np.cos(block_angle), -np.sin(block_angle)], axis=0).T * scale
    turn = 2.0 * np.pi / period * np.outer(half, np.arange(rows))
    row_angle = 2.0 * np.pi / rows * np.outer(np.arange(rows), np.arange(rows))
    row_cos, row_sin = np.cos(row_angle), np.sin(row_angle)
    forward = np.block([[row_cos, -row_sin], [row_sin, row_cos]])
    inverse = np.block([[row_cos, row_sin], [-row_sin, row_cos]])
    enter_high, enter_low = split_pair(enter)
    leave_high, leave_low = split_pair(leave)
    return (
        np.concatenate([enter_high, enter_low], axis=1),
        np.concatenate([leave_high, leave_low, leave_high], axis=1),
        *(
            np.concatenate([high, low, high], axis=0)
            for high, low in (split_pair(forward), split_pair(inverse))
        ),
        np.cos(turn).astype(np.float32),
        np.sin(turn).astype(np.float32),
    )


def split_value(x):
    high = x.astype(BF16)
    return high, (x - high.astype(F32)).astype(BF16)


def dot(a, b):
    return jnp.dot(a, b, preferred_element_type=F32)


def triple(x, axis):
    high, low = split_value(x)
    return jnp.concatenate([high, high, low], axis=axis)


def dot_rows(x, table):
    size = x.shape[0] // PIECES
    parts = [dot(triple(x[k * size : (k + 1) * size], 1), table) for k in range(PIECES)]
    return jnp.concatenate(parts, axis=0)


def pack_kernel(rank_ref, values_ref, gates_ref, grad_ref, filter_ref, out_ref, values, gates, grad, taps, rows_ref, sems):
    pairs = rows_ref.shape[0] // LINES
    copies = [
        pltpu.make_async_copy(src, dst, sems.at[k])
        for k, (src, dst) in enumerate(
            ((values_ref, values), (filter_ref, taps), (gates_ref, gates), (grad_ref, grad))
        )
    ]
    for copy in copies:
        copy.start()

    def put(line, rows):
        rows_ref[pl.ds(line, pairs, stride=LINES), :] = rows

    def place(part, first):
        turned = part.T
        for q in range(SHARE):
            put(first + q, turned[q * pairs : (q + 1) * pairs, :])

    copies[0].wait()
    place(values[...].astype(F32), 0)
    copies[1].wait()
    start = pl.multiple_of(rank_ref[0] * pairs, pairs)
    own = taps[:, pl.ds(start, pairs)].astype(F32).T
    for line in range(2 * SHARE, LINES):
        put(line, own)
    copies[2].wait()
    copies[3].wait()
    gate_term = (grad[...] * gates[...].astype(F32)).astype(BF16).astype(F32)
    place(gate_term, SHARE)
    out_ref[...] = rows_ref[...].astype(BF16)


def spectra_kernel(
    in_ref, enter_ref, leave_ref, forward_ref, inverse_ref, cos_ref, sin_ref, out_ref, wide, result
):
    blocks, rows = cos_ref.shape
    copies = in_ref.shape[0] // (blocks * LINES)
    cos_t, sin_t = cos_ref[...], sin_ref[...]
    wide[...] = in_ref[...].astype(F32)

    def spectrum(starts):
        cols = [wide[pl.ds(start, blocks, stride=LINES), :] for start in starts]
        joined = jnp.concatenate(cols, axis=1).astype(BF16)
        mixed = dot(enter_ref[...], jnp.concatenate([joined, joined], axis=0))
        turned = []
        for c in range(len(starts)):
            re = mixed[:blocks, c * rows : (c + 1) * rows]
            im = mixed[blocks:, c * rows : (c + 1) * rows]
            turned.append(
                jnp.concatenate([re * cos_t + im * sin_t, im * cos_t - re * sin_t], axis=1)
            )
        full = dot_rows(jnp.concatenate(turned, axis=0), forward_ref[...])
        return full[:, :rows], full[:, rows:]

    def signal(re, im):
        full = dot_rows(jnp.concatenate([re, im], axis=1), inverse_ref[...])
        cols = []
        for c in range(full.shape[0] // blocks):
            re = full[c * blocks : (c + 1) * blocks, :rows]
            im = full[c * blocks : (c + 1) * blocks, rows:]
            cols.append(
                jnp.concatenate([re * cos_t - im * sin_t, re * sin_t + im * cos_t], axis=0)
            )
        mixed = dot(leave_ref[...], triple(jnp.concatenate(cols, axis=1), 0))
        return [mixed[:, c * rows : (c + 1) * rows] for c in range(len(cols))]

    def put(block, line, col):
        result[pl.ds(block * blocks * LINES + line, blocks, stride=LINES), :] = col

    pairs = [(j, q) for j in range(copies) for q in range(SHARE)]
    size, part = len(pairs) * blocks, SHARE * blocks
    re, im = spectrum(
        [j * blocks * LINES + q for j, q in pairs]
        + [j * blocks * LINES + SHARE + q for j, q in pairs]
        + [q * blocks * LINES + 2 * SHARE for q in range(SHARE)]
    )
    v_re, v_im, g_re, g_im = re[:size], im[:size], re[size : 2 * size], im[size : 2 * size]
    h_re = jnp.concatenate([re[2 * size :]] * copies, axis=0)
    h_im = jnp.concatenate([im[2 * size :]] * copies, axis=0)
    f_re, f_im = v_re * g_re + v_im * g_im, v_re * g_im - v_im * g_re
    f_re = sum(f_re[j * part : (j + 1) * part] for j in range(copies))
    f_im = sum(f_im[j * part : (j + 1) * part] for j in range(copies))
    cols = signal(
        jnp.concatenate([h_re * v_re - h_im * v_im, h_re * g_re + h_im * g_im, f_re], axis=0),
        jnp.concatenate([h_re * v_im + h_im * v_re, h_re * g_im - h_im * g_re, f_im], axis=0),
    )
    for k, (j, q) in enumerate(pairs):
        put(j, q, cols[k])
        put(j, SHARE + q, cols[len(pairs) + k])
    for j in range(SHARE):
        for line in range(2 * SHARE, LINES):
            put(j, line, cols[2 * len(pairs) + j])
    out_ref[...] = result[...].astype(BF16)


def finish_kernel(
    values_ref, gates_ref, grad_ref, skip_ref, in_ref, value_out, gate_out, filter_out, wide, flat
):
    pairs = flat.shape[0] // SHARE
    wide[...] = in_ref[...].astype(F32)

    def part(first):
        for q in range(SHARE):
            flat[q * pairs : (q + 1) * pairs, :] = wide[
                pl.ds(first + q, pairs, stride=LINES), :
            ]
        return flat[...].T

    grad = grad_ref[...]
    skip = skip_ref[...]
    gate_out[...] = (grad * (part(0) + skip * values_ref[...].astype(F32))).astype(BF16)
    gate_term = (grad * gates_ref[...].astype(F32)).astype(BF16).astype(F32)
    value_out[...] = (part(SHARE) + skip * gate_term).astype(BF16)
    filter_out[...] = wide[pl.ds(2 * SHARE, pairs, stride=LINES), :].T


def call(kernel, out_shape, args, scratch, specs=None, limit=48):
    return pl.pallas_call(
        kernel,
        out_shape=out_shape,
        in_specs=specs or [VMEM] * len(args),
        out_specs=jax.tree.map(lambda _: VMEM, out_shape),
        scratch_shapes=scratch,
        compiler_params=pltpu.CompilerParams(vmem_limit_bytes=limit * 1024 * 1024),
    )(*args)


def exchange(x):
    shaped = x.reshape(lax.axis_size("chan") * lax.axis_size("seq"), -1, 2, x.shape[1])
    moved = lax.all_to_all(shaped, ("chan", "seq"), split_axis=0, concat_axis=0, tiled=True)
    return moved.reshape(x.shape)


def transform(held, blocks):
    rows = held.shape[1]
    consts = tables(blocks, rows)
    return call(
        spectra_kernel,
        jax.ShapeDtypeStruct(held.shape, BF16),
        (held, *consts),
        [pltpu.VMEM(held.shape, F32), pltpu.VMEM(held.shape, F32)],
    )


def local(values, gates, grad_out, filter_raw, skip_gain):
    rows, width = values.shape
    blocks = lax.axis_size("seq")
    pairs = blocks * lax.axis_size("chan")
    rank = lax.axis_index("chan").astype(jnp.int32).reshape(1)
    flat = pltpu.VMEM((width, rows), F32)
    scalar = pl.BlockSpec(memory_space=pltpu.SMEM)
    sent = call(
        pack_kernel,
        jax.ShapeDtypeStruct((pairs * LINES, rows), BF16),
        (rank, values, gates, grad_out, filter_raw),
        [
            pltpu.VMEM((rows, width), BF16),
            pltpu.VMEM((rows, width), BF16),
            pltpu.VMEM((rows, width), F32),
            pltpu.VMEM((rows, width), BF16),
            pltpu.VMEM((pairs * LINES, rows), F32),
            pltpu.SemaphoreType.DMA((4,)),
        ],
        [scalar] + [pl.BlockSpec(memory_space=pltpu.HBM)] * 4,
        limit=60,
    )
    back = exchange(transform(exchange(sent), blocks))
    shape = jax.ShapeDtypeStruct((rows, width), BF16)
    return call(
        finish_kernel,
        (shape, shape, jax.ShapeDtypeStruct((rows, width // lax.axis_size("chan")), F32)),
        (values, gates, grad_out, skip_gain[None, :], back),
        [pltpu.VMEM(back.shape, F32), flat],
    )


def solution(mesh):
    in_specs = (P("seq", "chan"), P("seq", "chan"), P("seq", "chan"), P("seq", None), P("chan"))
    out_specs = (P("seq", "chan"), P("seq", "chan"), P("seq", "chan"))
    return jax.shard_map(local, mesh=mesh, in_specs=in_specs, out_specs=out_specs, check_vma=False)
```

```python
import math

import jax
import jax.numpy as jnp
import numpy as np
from jax import lax
from jax.experimental import pallas as pl
from jax.experimental.pallas import tpu as pltpu
from jax.sharding import PartitionSpec as P

F32 = jnp.float32
BF16 = jnp.bfloat16
VMEM = pl.BlockSpec(memory_space=pltpu.VMEM)
SHARE = 4
PIECES = 4
LINES = 10


def split_pair(table):
    high = table.astype(np.float32).astype(jnp.bfloat16)
    low = (table - high.astype(np.float64)).astype(np.float32).astype(jnp.bfloat16)
    return high, low


def tables(blocks, rows):
    period = 2 * blocks * rows
    scale = 2.0 / period / math.sqrt(blocks * rows)
    half = np.arange(blocks) + 0.5
    block_angle = 2.0 * np.pi / (2 * blocks) * np.outer(half, np.arange(blocks))
    enter = np.concatenate([np.cos(block_angle), -np.sin(block_angle)], axis=0)
    leave = np.concatenate([np.cos(block_angle), -np.sin(block_angle)], axis=0).T * scale
    turn = 2.0 * np.pi / period * np.outer(half, np.arange(rows))
    row_angle = 2.0 * np.pi / rows * np.outer(np.arange(rows), np.arange(rows))
    row_cos, row_sin = np.cos(row_angle), np.sin(row_angle)
    forward = np.block([[row_cos, -row_sin], [row_sin, row_cos]])
    inverse = np.block([[row_cos, row_sin], [-row_sin, row_cos]])
    enter_high, enter_low = split_pair(enter)
    leave_high, leave_low = split_pair(leave)
    return (
        np.concatenate([enter_high, enter_low], axis=1),
        np.concatenate([leave_high, leave_low, leave_high], axis=1),
        *(
            np.concatenate([high, low, high], axis=0)
            for high, low in (split_pair(forward), split_pair(inverse))
        ),
        np.cos(turn).astype(np.float32),
        np.sin(turn).astype(np.float32),
    )


def split_value(x):
    high = x.astype(BF16)
    return high, (x - high.astype(F32)).astype(BF16)


def dot(a, b):
    return jnp.dot(a, b, preferred_element_type=F32)


def triple(x, axis):
    high, low = split_value(x)
    return jnp.concatenate([high, high, low], axis=axis)


def dot_rows(x, table):
    size = x.shape[0] // PIECES
    parts = [dot(triple(x[k * size : (k + 1) * size], 1), table) for k in range(PIECES)]
    return jnp.concatenate(parts, axis=0)


def pack_kernel(rank_ref, values_ref, gates_ref, grad_ref, filter_ref, out_ref, values, gates, grad, taps, rows_ref, sems):
    pairs = out_ref.shape[0] // LINES
    copies = [
        pltpu.make_async_copy(src, dst, sems.at[k])
        for k, (src, dst) in enumerate(
            ((values_ref, values), (filter_ref, taps), (gates_ref, gates), (grad_ref, grad))
        )
    ]
    for copy in copies:
        copy.start()

    def put(line, rows):
        rows_ref[pl.ds(line, pairs, stride=LINES), :] = rows

    def place(part, first):
        turned = part.T
        for q in range(SHARE):
            put(first + q, turned[q * pairs : (q + 1) * pairs, :])

    copies[0].wait()
    place(values[...].astype(F32), 0)
    copies[1].wait()
    start = pl.multiple_of(rank_ref[0] * pairs, pairs)
    own = taps[:, pl.ds(start, pairs)].astype(F32).T
    for line in range(2 * SHARE, LINES):
        put(line, own)
    copies[2].wait()
    copies[3].wait()
    gate_term = (grad[...] * gates[...].astype(F32)).astype(BF16).astype(F32)
    place(gate_term, SHARE)
    out_ref[...] = rows_ref[: out_ref.shape[0], :].astype(BF16)


def spectra_kernel(
    in_ref, enter_ref, leave_ref, forward_ref, inverse_ref, cos_ref, sin_ref, out_ref, wide, result
):
    blocks, rows = cos_ref.shape
    copies = in_ref.shape[0] // (blocks * LINES)
    cos_t, sin_t = cos_ref[...], sin_ref[...]
    wide[: in_ref.shape[0], :] = in_ref[...].astype(F32)

    def spectrum(starts):
        cols = [wide[pl.ds(start, blocks, stride=LINES), :] for start in starts]
        joined = jnp.concatenate(cols, axis=1).astype(BF16)
        mixed = dot(enter_ref[...], jnp.concatenate([joined, joined], axis=0))
        turned = []
        for c in range(len(starts)):
            re = mixed[:blocks, c * rows : (c + 1) * rows]
            im = mixed[blocks:, c * rows : (c + 1) * rows]
            turned.append(
                jnp.concatenate([re * cos_t + im * sin_t, im * cos_t - re * sin_t], axis=1)
            )
        full = dot_rows(jnp.concatenate(turned, axis=0), forward_ref[...])
        return full[:, :rows], full[:, rows:]

    def signal(re, im):
        full = dot_rows(jnp.concatenate([re, im], axis=1), inverse_ref[...])
        cols = []
        for c in range(full.shape[0] // blocks):
            re = full[c * blocks : (c + 1) * blocks, :rows]
            im = full[c * blocks : (c + 1) * blocks, rows:]
            cols.append(
                jnp.concatenate([re * cos_t - im * sin_t, re * sin_t + im * cos_t], axis=0)
            )
        mixed = dot(leave_ref[...], triple(jnp.concatenate(cols, axis=1), 0))
        return [mixed[:, c * rows : (c + 1) * rows] for c in range(len(cols))]

    def put(block, line, col):
        result[pl.ds(block * blocks * LINES + line, blocks, stride=LINES), :] = col

    pairs = [(j, q) for j in range(copies) for q in range(SHARE)]
    size, part = len(pairs) * blocks, SHARE * blocks
    re, im = spectrum(
        [j * blocks * LINES + q for j, q in pairs]
        + [j * blocks * LINES + SHARE + q for j, q in pairs]
        + [q * blocks * LINES + 2 * SHARE for q in range(SHARE)]
    )
    v_re, v_im, g_re, g_im = re[:size], im[:size], re[size : 2 * size], im[size : 2 * size]
    h_re = jnp.concatenate([re[2 * size :]] * copies, axis=0)
    h_im = jnp.concatenate([im[2 * size :]] * copies, axis=0)
    f_re, f_im = v_re * g_re + v_im * g_im, v_re * g_im - v_im * g_re
    f_re = sum(f_re[j * part : (j + 1) * part] for j in range(copies))
    f_im = sum(f_im[j * part : (j + 1) * part] for j in range(copies))
    cols = signal(
        jnp.concatenate([h_re * v_re - h_im * v_im, h_re * g_re + h_im * g_im, f_re], axis=0),
        jnp.concatenate([h_re * v_im + h_im * v_re, h_re * g_im - h_im * g_re, f_im], axis=0),
    )
    for k, (j, q) in enumerate(pairs):
        put(j, q, cols[k])
        put(j, SHARE + q, cols[len(pairs) + k])
    for j in range(SHARE):
        for line in range(2 * SHARE, LINES):
            put(j, line, cols[2 * len(pairs) + j])
    out_ref[...] = result[: out_ref.shape[0], :].astype(BF16)


def finish_kernel(
    values_ref, gates_ref, grad_ref, skip_ref, in_ref, value_out, gate_out, filter_out, wide, flat
):
    pairs = flat.shape[0] // SHARE
    wide[: in_ref.shape[0], :] = in_ref[...].astype(F32)

    def part(first):
        for q in range(SHARE):
            flat[q * pairs : (q + 1) * pairs, :] = wide[
                pl.ds(first + q, pairs, stride=LINES), :
            ]
        return flat[...].T

    grad = grad_ref[...]
    skip = skip_ref[...]
    gate_out[...] = (grad * (part(0) + skip * values_ref[...].astype(F32))).astype(BF16)
    gate_term = (grad * gates_ref[...].astype(F32)).astype(BF16).astype(F32)
    value_out[...] = (part(SHARE) + skip * gate_term).astype(BF16)
    filter_out[...] = wide[pl.ds(2 * SHARE, pairs, stride=LINES), :].T


def call(kernel, out_shape, args, scratch, specs=None, limit=48):
    return pl.pallas_call(
        kernel,
        out_shape=out_shape,
        in_specs=specs or [VMEM] * len(args),
        out_specs=jax.tree.map(lambda _: VMEM, out_shape),
        scratch_shapes=scratch,
        compiler_params=pltpu.CompilerParams(vmem_limit_bytes=limit * 1024 * 1024),
    )(*args)


def spare(x):
    return pltpu.VMEM((x.shape[0] + 16, x.shape[1]), F32)


def exchange(x):
    shaped = x.reshape(lax.axis_size("chan") * lax.axis_size("seq"), -1, 2, x.shape[1])
    moved = lax.all_to_all(shaped, ("chan", "seq"), split_axis=0, concat_axis=0, tiled=True)
    return moved.reshape(x.shape)


def transform(held, blocks):
    rows = held.shape[1]
    consts = tables(blocks, rows)
    return call(
        spectra_kernel,
        jax.ShapeDtypeStruct(held.shape, BF16),
        (held, *consts),
        [spare(held), spare(held)],
    )


def local(values, gates, grad_out, filter_raw, skip_gain):
    rows, width = values.shape
    blocks = lax.axis_size("seq")
    pairs = blocks * lax.axis_size("chan")
    rank = lax.axis_index("chan").astype(jnp.int32).reshape(1)
    flat = pltpu.VMEM((width, rows), F32)
    scalar = pl.BlockSpec(memory_space=pltpu.SMEM)
    sent = jax.ShapeDtypeStruct((pairs * LINES, rows), BF16)
    sent = call(
        pack_kernel,
        sent,
        (rank, values, gates, grad_out, filter_raw),
        [
            pltpu.VMEM((rows, width), BF16),
            pltpu.VMEM((rows, width), BF16),
            pltpu.VMEM((rows, width), F32),
            pltpu.VMEM((rows, width), BF16),
            spare(sent),
            pltpu.SemaphoreType.DMA((4,)),
        ],
        [scalar] + [pl.BlockSpec(memory_space=pltpu.HBM)] * 4,
        limit=60,
    )
    back = exchange(transform(exchange(sent), blocks))
    shape = jax.ShapeDtypeStruct((rows, width), BF16)
    return call(
        finish_kernel,
        (shape, shape, jax.ShapeDtypeStruct((rows, width // lax.axis_size("chan")), F32)),
        (values, gates, grad_out, skip_gain[None, :], back),
        [spare(back), flat],
    )


def solution(mesh):
    in_specs = (P("seq", "chan"), P("seq", "chan"), P("seq", "chan"), P("seq", None), P("chan"))
    out_specs = (P("seq", "chan"), P("seq", "chan"), P("seq", "chan"))
    return jax.shard_map(local, mesh=mesh, in_specs=in_specs, out_specs=out_specs, check_vma=False)
```

```python
import math

import jax
import jax.numpy as jnp
import numpy as np
from jax import lax
from jax.experimental import pallas as pl
from jax.experimental.pallas import tpu as pltpu
from jax.sharding import PartitionSpec as P

F32 = jnp.float32
BF16 = jnp.bfloat16
VMEM = pl.BlockSpec(memory_space=pltpu.VMEM)
SHARE = 4
PIECES = 4
LINES = 10


def split_pair(table):
    high = table.astype(np.float32).astype(jnp.bfloat16)
    low = (table - high.astype(np.float64)).astype(np.float32).astype(jnp.bfloat16)
    return high, low


def tables(blocks, rows):
    period = 2 * blocks * rows
    scale = 2.0 / period / math.sqrt(blocks * rows)
    half = np.arange(blocks) + 0.5
    block_angle = 2.0 * np.pi / (2 * blocks) * np.outer(half, np.arange(blocks))
    enter = np.concatenate([np.cos(block_angle), -np.sin(block_angle)], axis=0)
    leave = np.concatenate([np.cos(block_angle), -np.sin(block_angle)], axis=0).T * scale
    turn = 2.0 * np.pi / period * np.outer(half, np.arange(rows))
    row_angle = 2.0 * np.pi / rows * np.outer(np.arange(rows), np.arange(rows))
    row_cos, row_sin = np.cos(row_angle), np.sin(row_angle)
    forward = np.block([[row_cos, -row_sin], [row_sin, row_cos]])
    inverse = np.block([[row_cos, row_sin], [-row_sin, row_cos]])
    enter_high, enter_low = split_pair(enter)
    leave_high, leave_low = split_pair(leave)
    return (
        np.concatenate([enter_high, enter_low], axis=1),
        np.block([[leave_high, leave_high], [leave_low, np.zeros_like(leave_low)]]),
        *(
            np.concatenate([high, low, high], axis=0)
            for high, low in (split_pair(forward), split_pair(inverse))
        ),
        np.cos(turn).astype(np.float32),
        np.sin(turn).astype(np.float32),
    )


def split_value(x):
    high = x.astype(BF16)
    return high, (x - high.astype(F32)).astype(BF16)


def dot(a, b):
    return jnp.dot(a, b, preferred_element_type=F32)


def triple(x, axis):
    high, low = split_value(x)
    return jnp.concatenate([high, high, low], axis=axis)


def dot_rows(x, table):
    size = x.shape[0] // PIECES
    parts = [dot(triple(x[k * size : (k + 1) * size], 1), table) for k in range(PIECES)]
    return jnp.concatenate(parts, axis=0)


def pack_kernel(rank_ref, values_ref, gates_ref, grad_ref, filter_ref, out_ref, values, gates, grad, taps, rows_ref, sems):
    pairs = out_ref.shape[0] // LINES
    copies = [
        pltpu.make_async_copy(src, dst, sems.at[k])
        for k, (src, dst) in enumerate(
            ((values_ref, values), (filter_ref, taps), (gates_ref, gates), (grad_ref, grad))
        )
    ]
    for copy in copies:
        copy.start()

    def put(line, rows):
        rows_ref[pl.ds(line, pairs, stride=LINES), :] = rows

    def place(part, first):
        turned = part.T
        for q in range(SHARE):
            put(first + q, turned[q * pairs : (q + 1) * pairs, :])

    copies[0].wait()
    place(values[...].astype(F32), 0)
    copies[1].wait()
    start = pl.multiple_of(rank_ref[0] * pairs, pairs)
    own = taps[:, pl.ds(start, pairs)].astype(F32).T
    for line in range(2 * SHARE, LINES):
        put(line, own)
    copies[2].wait()
    copies[3].wait()
    gate_term = (grad[...] * gates[...].astype(F32)).astype(BF16).astype(F32)
    place(gate_term, SHARE)
    out_ref[...] = rows_ref[: out_ref.shape[0], :].astype(BF16)


def spectra_kernel(
    in_ref, enter_ref, leave_ref, forward_ref, inverse_ref, cos_ref, sin_ref, out_ref, wide, result
):
    blocks, rows = cos_ref.shape
    copies = in_ref.shape[0] // (blocks * LINES)
    cos_t, sin_t = cos_ref[...], sin_ref[...]
    wide[: in_ref.shape[0], :] = in_ref[...].astype(F32)

    def spectrum(starts):
        table = forward_ref[...]
        step = len(starts) // PIECES

        def turn(first):
            cols = [wide[pl.ds(start, blocks, stride=LINES), :] for start in starts[first : first + step]]
            joined = jnp.concatenate(cols, axis=1).astype(BF16)
            mixed = dot(enter_ref[...], jnp.concatenate([joined, joined], axis=0))
            turned = []
            for c in range(step):
                re = mixed[:blocks, c * rows : (c + 1) * rows]
                im = mixed[blocks:, c * rows : (c + 1) * rows]
                turned.append(
                    jnp.concatenate([re * cos_t + im * sin_t, im * cos_t - re * sin_t], axis=1)
                )
            return triple(jnp.concatenate(turned, axis=0), 1)

        full = []
        ready = turn(0)
        for first in range(0, len(starts), step):
            ahead = turn(first + step) if first + step < len(starts) else None
            full.append(dot(ready, table))
            ready = ahead
        full = jnp.concatenate(full, axis=0)
        return full[:, :rows], full[:, rows:]

    def signal(re, im):
        table = inverse_ref[...]
        size = re.shape[0] // 4
        starts = list(range(0, re.shape[0], size))

        def product(k):
            return dot(triple(jnp.concatenate([re[k : k + size], im[k : k + size]], axis=1), 1), table)

        def turn(full):
            cols = []
            for c in range(0, size, blocks):
                x, y = full[c : c + blocks, :rows], full[c : c + blocks, rows:]
                cols.append(jnp.concatenate([x * cos_t - y * sin_t, x * sin_t + y * cos_t], axis=0))
            return jnp.concatenate(split_value(jnp.concatenate(cols, axis=1)), axis=0)

        waiting, done = [], []

        def leave(x):
            both = dot(leave_ref[...], x)
            mixed = both[:blocks] + both[blocks:]
            return [mixed[:, c : c + rows] for c in range(0, mixed.shape[1], rows)]

        held = []
        for k in starts:
            waiting.append(product(k))
            if len(waiting) > 1:
                held.append(turn(waiting.pop(0)))
        while waiting:
            held.append(turn(waiting.pop(0)))
        for x in held:
            done += leave(x)
        return done

    def put(block, line, col):
        result[pl.ds(block * blocks * LINES + line, blocks, stride=LINES), :] = col

    pairs = [(j, q) for j in range(copies) for q in range(SHARE)]
    size, part = len(pairs) * blocks, SHARE * blocks
    re, im = spectrum(
        [j * blocks * LINES + q for j, q in pairs]
        + [j * blocks * LINES + SHARE + q for j, q in pairs]
        + [q * blocks * LINES + 2 * SHARE for q in range(SHARE)]
    )
    v_re, v_im, g_re, g_im = re[:size], im[:size], re[size : 2 * size], im[size : 2 * size]
    h_re = jnp.concatenate([re[2 * size :]] * copies, axis=0)
    h_im = jnp.concatenate([im[2 * size :]] * copies, axis=0)
    f_re, f_im = v_re * g_re + v_im * g_im, v_re * g_im - v_im * g_re
    f_re = sum(f_re[j * part : (j + 1) * part] for j in range(copies))
    f_im = sum(f_im[j * part : (j + 1) * part] for j in range(copies))
    cols = signal(
        jnp.concatenate([h_re * v_re - h_im * v_im, h_re * g_re + h_im * g_im, f_re], axis=0),
        jnp.concatenate([h_re * v_im + h_im * v_re, h_re * g_im - h_im * g_re, f_im], axis=0),
    )
    for k, (j, q) in enumerate(pairs):
        put(j, q, cols[k])
        put(j, SHARE + q, cols[len(pairs) + k])
    for j in range(SHARE):
        for line in range(2 * SHARE, LINES):
            put(j, line, cols[2 * len(pairs) + j])
    out_ref[...] = result[: out_ref.shape[0], :].astype(BF16)


def finish_kernel(
    values_ref, gates_ref, grad_ref, skip_ref, in_ref, value_out, gate_out, filter_out, wide, flat
):
    pairs = flat.shape[0] // SHARE
    wide[: in_ref.shape[0], :] = in_ref[...].astype(F32)

    def part(first):
        for q in range(SHARE):
            flat[q * pairs : (q + 1) * pairs, :] = wide[
                pl.ds(first + q, pairs, stride=LINES), :
            ]
        return flat[...].T

    grad = grad_ref[...]
    skip = skip_ref[...]
    gate_out[...] = (grad * (part(0) + skip * values_ref[...].astype(F32))).astype(BF16)
    gate_term = (grad * gates_ref[...].astype(F32)).astype(BF16).astype(F32)
    value_out[...] = (part(SHARE) + skip * gate_term).astype(BF16)
    filter_out[...] = wide[pl.ds(2 * SHARE, pairs, stride=LINES), :].T


def call(kernel, out_shape, args, scratch, specs=None, limit=48):
    return pl.pallas_call(
        kernel,
        out_shape=out_shape,
        in_specs=specs or [VMEM] * len(args),
        out_specs=jax.tree.map(lambda _: VMEM, out_shape),
        scratch_shapes=scratch,
        compiler_params=pltpu.CompilerParams(vmem_limit_bytes=limit * 1024 * 1024),
    )(*args)


def spare(x):
    return pltpu.VMEM((x.shape[0] + 16, x.shape[1]), F32)


def exchange(x):
    shaped = x.reshape(lax.axis_size("chan") * lax.axis_size("seq"), -1, 2, x.shape[1])
    moved = lax.all_to_all(shaped, ("chan", "seq"), split_axis=0, concat_axis=0, tiled=True)
    return moved.reshape(x.shape)


def transform(held, blocks):
    rows = held.shape[1]
    consts = tables(blocks, rows)
    return call(
        spectra_kernel,
        jax.ShapeDtypeStruct(held.shape, BF16),
        (held, *consts),
        [spare(held), spare(held)],
    )


def local(values, gates, grad_out, filter_raw, skip_gain):
    rows, width = values.shape
    blocks = lax.axis_size("seq")
    pairs = blocks * lax.axis_size("chan")
    rank = lax.axis_index("chan").astype(jnp.int32).reshape(1)
    flat = pltpu.VMEM((width, rows), F32)
    scalar = pl.BlockSpec(memory_space=pltpu.SMEM)
    sent = jax.ShapeDtypeStruct((pairs * LINES, rows), BF16)
    sent = call(
        pack_kernel,
        sent,
        (rank, values, gates, grad_out, filter_raw),
        [
            pltpu.VMEM((rows, width), BF16),
            pltpu.VMEM((rows, width), BF16),
            pltpu.VMEM((rows, width), F32),
            pltpu.VMEM((rows, width), BF16),
            spare(sent),
            pltpu.SemaphoreType.DMA((4,)),
        ],
        [scalar] + [pl.BlockSpec(memory_space=pltpu.HBM)] * 4,
        limit=60,
    )
    back = exchange(transform(exchange(sent), blocks))
    shape = jax.ShapeDtypeStruct((rows, width), BF16)
    return call(
        finish_kernel,
        (shape, shape, jax.ShapeDtypeStruct((rows, width // lax.axis_size("chan")), F32)),
        (values, gates, grad_out, skip_gain[None, :], back),
        [spare(back), flat],
    )


def solution(mesh):
    in_specs = (P("seq", "chan"), P("seq", "chan"), P("seq", "chan"), P("seq", None), P("chan"))
    out_specs = (P("seq", "chan"), P("seq", "chan"), P("seq", "chan"))
    return jax.shard_map(local, mesh=mesh, in_specs=in_specs, out_specs=out_specs, check_vma=False)
```

```python
import math

import jax
import jax.numpy as jnp
import numpy as np
from jax import lax
from jax.experimental import pallas as pl
from jax.experimental.pallas import tpu as pltpu
from jax.sharding import PartitionSpec as P

F32 = jnp.float32
BF16 = jnp.bfloat16
VMEM = pl.BlockSpec(memory_space=pltpu.VMEM)
SHARE = 4
PIECES = 4
LINES = 10


def split_pair(table):
    high = table.astype(np.float32).astype(jnp.bfloat16)
    low = (table - high.astype(np.float64)).astype(np.float32).astype(jnp.bfloat16)
    return high, low


def tables(blocks, rows):
    period = 2 * blocks * rows
    scale = 2.0 / period / math.sqrt(blocks * rows)
    half = np.arange(blocks) + 0.5
    block_angle = 2.0 * np.pi / (2 * blocks) * np.outer(half, np.arange(blocks))
    enter = np.concatenate([np.cos(block_angle), -np.sin(block_angle)], axis=0)
    leave = np.concatenate([np.cos(block_angle), -np.sin(block_angle)], axis=0).T * scale
    turn = 2.0 * np.pi / period * np.outer(half, np.arange(rows))
    row_angle = 2.0 * np.pi / rows * np.outer(np.arange(rows), np.arange(rows))
    row_cos, row_sin = np.cos(row_angle), np.sin(row_angle)
    forward = np.block([[row_cos, -row_sin], [row_sin, row_cos]])
    inverse = np.block([[row_cos, row_sin], [-row_sin, row_cos]])
    enter_high, enter_low = split_pair(enter)
    leave_high, leave_low = split_pair(leave)
    return (
        np.concatenate([enter_high, enter_low], axis=1),
        np.block([[leave_high, leave_high], [leave_low, np.zeros_like(leave_low)]]),
        *(
            np.concatenate([high, low, high], axis=0)
            for high, low in (split_pair(forward), split_pair(inverse))
        ),
        np.cos(turn).astype(np.float32),
        np.sin(turn).astype(np.float32),
    )


def split_value(x):
    high = x.astype(BF16)
    return high, (x - high.astype(F32)).astype(BF16)


def dot(a, b):
    return jnp.dot(a, b, preferred_element_type=F32)


def triple(x, axis):
    high, low = split_value(x)
    return jnp.concatenate([high, high, low], axis=axis)


def dot_rows(x, table):
    size = x.shape[0] // PIECES
    parts = [dot(triple(x[k * size : (k + 1) * size], 1), table) for k in range(PIECES)]
    return jnp.concatenate(parts, axis=0)


def pack_kernel(rank_ref, values_ref, gates_ref, grad_ref, filter_ref, out_ref, values, gates, grad, taps, rows_ref, sems):
    pairs = out_ref.shape[0] // LINES
    copies = [
        pltpu.make_async_copy(src, dst, sems.at[k])
        for k, (src, dst) in enumerate(
            ((values_ref, values), (filter_ref, taps), (gates_ref, gates), (grad_ref, grad))
        )
    ]
    for copy in copies:
        copy.start()

    def put(line, rows):
        rows_ref[pl.ds(line, pairs, stride=LINES), :] = rows

    def place(part, first):
        turned = part.T
        for q in range(SHARE):
            put(first + q, turned[q * pairs : (q + 1) * pairs, :])

    copies[0].wait()
    place(values[...].astype(F32), 0)
    copies[1].wait()
    start = pl.multiple_of(rank_ref[0] * pairs, pairs)
    own = taps[:, pl.ds(start, pairs)].astype(F32).T
    for line in range(2 * SHARE, LINES):
        put(line, own)
    copies[2].wait()
    copies[3].wait()
    gate_term = (grad[...] * gates[...].astype(F32)).astype(BF16).astype(F32)
    place(gate_term, SHARE)
    out_ref[...] = rows_ref[: out_ref.shape[0], :].astype(BF16)


def spectra_kernel(
    in_ref, enter_ref, leave_ref, forward_ref, inverse_ref, cos_ref, sin_ref, out_ref, wide, result
):
    blocks, rows = cos_ref.shape
    copies = in_ref.shape[0] // (blocks * LINES)
    cos_t, sin_t = cos_ref[...], sin_ref[...]
    wide[: in_ref.shape[0], :] = in_ref[...].astype(F32)

    def spectrum(starts):
        table = forward_ref[...]
        step = len(starts) // PIECES

        def turn(first):
            cols = [wide[pl.ds(start, blocks, stride=LINES), :] for start in starts[first : first + step]]
            joined = jnp.concatenate(cols, axis=1).astype(BF16)
            mixed = dot(enter_ref[...], jnp.concatenate([joined, joined], axis=0))
            turned = []
            for c in range(step):
                re = mixed[:blocks, c * rows : (c + 1) * rows]
                im = mixed[blocks:, c * rows : (c + 1) * rows]
                turned.append(
                    jnp.concatenate([re * cos_t + im * sin_t, im * cos_t - re * sin_t], axis=1)
                )
            return triple(jnp.concatenate(turned, axis=0), 1)

        full = []
        ready = turn(0)
        for first in range(0, len(starts), step):
            ahead = turn(first + step) if first + step < len(starts) else None
            full.append(dot(ready, table))
            ready = ahead
        full = jnp.concatenate(full, axis=0)
        return full[:, :rows], full[:, rows:]

    def signal(re, im):
        table = inverse_ref[...]
        size = re.shape[0] // 4
        starts = list(range(0, re.shape[0], size))

        def product(k):
            return dot(triple(jnp.concatenate([re[k : k + size], im[k : k + size]], axis=1), 1), table)

        def turn(full):
            cols = []
            for c in range(0, size, blocks):
                x, y = full[c : c + blocks, :rows], full[c : c + blocks, rows:]
                cols.append(jnp.concatenate([x * cos_t - y * sin_t, x * sin_t + y * cos_t], axis=0))
            return jnp.concatenate(split_value(jnp.concatenate(cols, axis=1)), axis=0)

        waiting, done = [], []

        def leave(x):
            both = dot(leave_ref[...], x)
            mixed = both[:blocks] + both[blocks:]
            return [mixed[:, c : c + rows] for c in range(0, mixed.shape[1], rows)]

        held = []
        for k in starts:
            waiting.append(product(k))
            if len(waiting) > 1:
                held.append(turn(waiting.pop(0)))
        while waiting:
            held.append(turn(waiting.pop(0)))
        for x in held:
            done += leave(x)
        return done

    def put(block, line, col):
        result[pl.ds(block * blocks * LINES + line, blocks, stride=LINES), :] = col

    pairs = [(j, q) for j in range(copies) for q in range(SHARE)]
    size, part = len(pairs) * blocks, SHARE * blocks
    re, im = spectrum(
        [j * blocks * LINES + q for j, q in pairs]
        + [j * blocks * LINES + SHARE + q for j, q in pairs]
        + [q * blocks * LINES + 2 * SHARE for q in range(SHARE)]
    )
    v_re, v_im, g_re, g_im = re[:size], im[:size], re[size : 2 * size], im[size : 2 * size]
    h_re = jnp.concatenate([re[2 * size :]] * copies, axis=0)
    h_im = jnp.concatenate([im[2 * size :]] * copies, axis=0)
    f_re, f_im = v_re * g_re + v_im * g_im, v_re * g_im - v_im * g_re
    f_re = sum(f_re[j * part : (j + 1) * part] for j in range(copies))
    f_im = sum(f_im[j * part : (j + 1) * part] for j in range(copies))
    cols = signal(
        jnp.concatenate([h_re * v_re - h_im * v_im, h_re * g_re + h_im * g_im, f_re], axis=0),
        jnp.concatenate([h_re * v_im + h_im * v_re, h_re * g_im - h_im * g_re, f_im], axis=0),
    )
    for k, (j, q) in enumerate(pairs):
        put(j, q, cols[k])
        put(j, SHARE + q, cols[len(pairs) + k])
    for j in range(SHARE):
        for line in range(2 * SHARE, LINES):
            put(j, line, cols[2 * len(pairs) + j])
    out_ref[...] = result[: out_ref.shape[0], :].astype(BF16)


def finish_kernel(
    values_ref, gates_ref, grad_ref, skip_ref, in_ref, value_out, gate_out, filter_out, wide, flat
):
    pairs = flat.shape[0] // SHARE
    wide[: in_ref.shape[0], :] = in_ref[...].astype(F32)

    def part(first):
        for q in range(SHARE):
            flat[q * pairs : (q + 1) * pairs, :] = wide[
                pl.ds(first + q, pairs, stride=LINES), :
            ]
        return flat[...].T

    grad = grad_ref[...]
    skip = skip_ref[...]
    gate_out[...] = (grad * (part(0) + skip * values_ref[...].astype(F32))).astype(BF16)
    gate_term = (grad * gates_ref[...].astype(F32)).astype(BF16).astype(F32)
    value_out[...] = (part(SHARE) + skip * gate_term).astype(BF16)
    filter_out[...] = wide[pl.ds(2 * SHARE, pairs, stride=LINES), :].T


def call(kernel, out_shape, args, scratch, specs=None, limit=48):
    return pl.pallas_call(
        kernel,
        out_shape=out_shape,
        in_specs=specs or [VMEM] * len(args),
        out_specs=jax.tree.map(lambda _: VMEM, out_shape),
        scratch_shapes=scratch,
        compiler_params=pltpu.CompilerParams(vmem_limit_bytes=limit * 1024 * 1024),
    )(*args)


def spare(x):
    return pltpu.VMEM((x.shape[0] + 16, x.shape[1]), F32)


def exchange(x):
    shaped = x.reshape(lax.axis_size("chan") * lax.axis_size("seq"), -1, 2, x.shape[1])
    moved = lax.all_to_all(shaped, ("chan", "seq"), split_axis=0, concat_axis=0, tiled=True)
    return moved.reshape(x.shape)


def transform(held, blocks):
    rows = held.shape[1]
    consts = tables(blocks, rows)
    return call(
        spectra_kernel,
        jax.ShapeDtypeStruct(held.shape, BF16),
        (held, *consts),
        [spare(held), spare(held)],
    )


def local(values, gates, grad_out, filter_raw, skip_gain):
    rows, width = values.shape
    blocks = lax.axis_size("seq")
    pairs = blocks * lax.axis_size("chan")
    rank = lax.axis_index("chan").astype(jnp.int32).reshape(1)
    flat = pltpu.VMEM((width, rows), F32)
    scalar = pl.BlockSpec(memory_space=pltpu.SMEM)
    sent = jax.ShapeDtypeStruct((pairs * LINES, rows), BF16)
    sent = call(
        pack_kernel,
        pltpu.VMEM(sent.shape, BF16),
        (rank, values, gates, grad_out, filter_raw),
        [
            pltpu.VMEM((rows, width), BF16),
            pltpu.VMEM((rows, width), BF16),
            pltpu.VMEM((rows, width), F32),
            pltpu.VMEM((rows, width), BF16),
            spare(sent),
            pltpu.SemaphoreType.DMA((4,)),
        ],
        [scalar] + [pl.BlockSpec(memory_space=pltpu.HBM)] * 4,
        limit=57,
    )
    back = exchange(transform(exchange(sent), blocks))
    shape = jax.ShapeDtypeStruct((rows, width), BF16)
    return call(
        finish_kernel,
        (shape, shape, jax.ShapeDtypeStruct((rows, width // lax.axis_size("chan")), F32)),
        (values, gates, grad_out, skip_gain[None, :], back),
        [spare(back), flat],
    )


def solution(mesh):
    in_specs = (P("seq", "chan"), P("seq", "chan"), P("seq", "chan"), P("seq", None), P("chan"))
    out_specs = (P("seq", "chan"), P("seq", "chan"), P("seq", "chan"))
    return jax.shard_map(local, mesh=mesh, in_specs=in_specs, out_specs=out_specs, check_vma=False)
```

```python
import math

import jax
import jax.numpy as jnp
import numpy as np
from jax import lax
from jax.experimental import pallas as pl
from jax.experimental.pallas import tpu as pltpu
from jax.sharding import PartitionSpec as P

F32 = jnp.float32
BF16 = jnp.bfloat16
VMEM = pl.BlockSpec(memory_space=pltpu.VMEM)
SHARE = 4
PIECES = 4
LINES = 10


def split_pair(table):
    high = table.astype(np.float32).astype(jnp.bfloat16)
    low = (table - high.astype(np.float64)).astype(np.float32).astype(jnp.bfloat16)
    return high, low


def tables(blocks, rows):
    period = 2 * blocks * rows
    scale = 2.0 / period / math.sqrt(blocks * rows)
    half = np.arange(blocks) + 0.5
    block_angle = 2.0 * np.pi / (2 * blocks) * np.outer(half, np.arange(blocks))
    enter = np.concatenate([np.cos(block_angle), -np.sin(block_angle)], axis=0)
    leave = np.concatenate([np.cos(block_angle), -np.sin(block_angle)], axis=0).T * scale
    turn = 2.0 * np.pi / period * np.outer(half, np.arange(rows))
    row_angle = 2.0 * np.pi / rows * np.outer(np.arange(rows), np.arange(rows))
    row_cos, row_sin = np.cos(row_angle), np.sin(row_angle)
    forward = np.block([[row_cos, -row_sin], [row_sin, row_cos]])
    inverse = np.block([[row_cos, row_sin], [-row_sin, row_cos]])
    enter_high, enter_low = split_pair(enter)
    leave_high, leave_low = split_pair(leave)
    wide = [
        np.concatenate([high, low, high], axis=0)
        for high, low in (split_pair(forward), split_pair(inverse))
    ]
    wide.append(np.block([[leave_high, leave_high], [leave_low, np.zeros_like(leave_low)]]))
    turns = np.concatenate([np.cos(turn), np.sin(turn)], axis=0).astype(np.float32)
    return np.concatenate([enter_high, enter_low], axis=1), np.concatenate(wide, axis=0), turns


def split_value(x):
    high = x.astype(BF16)
    return high, (x - high.astype(F32)).astype(BF16)


def dot(a, b):
    return jnp.dot(a, b, preferred_element_type=F32)


def triple(x, axis):
    high, low = split_value(x)
    return jnp.concatenate([high, high, low], axis=axis)


def dot_rows(x, table):
    size = x.shape[0] // PIECES
    parts = [dot(triple(x[k * size : (k + 1) * size], 1), table) for k in range(PIECES)]
    return jnp.concatenate(parts, axis=0)


def pack_kernel(rank_ref, values_ref, gates_ref, grad_ref, filter_ref, out_ref, values, gates, grad, taps, rows_ref, sems):
    pairs = out_ref.shape[0] // LINES
    copies = [
        pltpu.make_async_copy(src, dst, sems.at[k])
        for k, (src, dst) in enumerate(
            ((values_ref, values), (filter_ref, taps), (gates_ref, gates), (grad_ref, grad))
        )
    ]
    for copy in copies:
        copy.start()

    def put(line, rows):
        rows_ref[pl.ds(line, pairs, stride=LINES), :] = rows

    def place(part, first):
        turned = part.T
        for q in range(SHARE):
            put(first + q, turned[q * pairs : (q + 1) * pairs, :])

    copies[0].wait()
    place(values[...].astype(F32), 0)
    copies[1].wait()
    start = pl.multiple_of(rank_ref[0] * pairs, pairs)
    own = taps[:, pl.ds(start, pairs)].astype(F32).T
    for line in range(2 * SHARE, LINES):
        put(line, own)
    copies[2].wait()
    copies[3].wait()
    gate_term = (grad[...] * gates[...].astype(F32)).astype(BF16).astype(F32)
    place(gate_term, SHARE)
    out_ref[...] = rows_ref[: out_ref.shape[0], :].astype(BF16)


def spectra_kernel(
    in_ref, enter_ref, table_ref, turn_ref, out_ref, wide, result
):
    blocks, rows = turn_ref.shape[0] // 2, turn_ref.shape[1]
    deep = 6 * rows
    copies = in_ref.shape[0] // (blocks * LINES)
    cos_t, sin_t = turn_ref[:blocks, :], turn_ref[blocks:, :]
    wide[: in_ref.shape[0], :] = in_ref[...].astype(F32)

    def spectrum(starts):
        table = table_ref[:deep, :]
        step = len(starts) // PIECES

        def turn(first):
            cols = [wide[pl.ds(start, blocks, stride=LINES), :] for start in starts[first : first + step]]
            joined = jnp.concatenate(cols, axis=1).astype(BF16)
            mixed = dot(enter_ref[...], jnp.concatenate([joined, joined], axis=0))
            turned = []
            for c in range(step):
                re = mixed[:blocks, c * rows : (c + 1) * rows]
                im = mixed[blocks:, c * rows : (c + 1) * rows]
                turned.append(
                    jnp.concatenate([re * cos_t + im * sin_t, im * cos_t - re * sin_t], axis=1)
                )
            return triple(jnp.concatenate(turned, axis=0), 1)

        full = []
        ready = turn(0)
        for first in range(0, len(starts), step):
            ahead = turn(first + step) if first + step < len(starts) else None
            full.append(dot(ready, table))
            ready = ahead
        full = jnp.concatenate(full, axis=0)
        return full[:, :rows], full[:, rows:]

    def signal(re, im):
        table = table_ref[deep : 2 * deep, :]
        size = re.shape[0] // 4
        starts = list(range(0, re.shape[0], size))

        def product(k):
            return dot(triple(jnp.concatenate([re[k : k + size], im[k : k + size]], axis=1), 1), table)

        def turn(full):
            cols = []
            for c in range(0, size, blocks):
                x, y = full[c : c + blocks, :rows], full[c : c + blocks, rows:]
                cols.append(jnp.concatenate([x * cos_t - y * sin_t, x * sin_t + y * cos_t], axis=0))
            return jnp.concatenate(split_value(jnp.concatenate(cols, axis=1)), axis=0)

        waiting, done = [], []

        def leave(x):
            both = dot(table_ref[2 * deep :, :], x)
            mixed = both[:blocks] + both[blocks:]
            return [mixed[:, c : c + rows] for c in range(0, mixed.shape[1], rows)]

        held = []
        for k in starts:
            waiting.append(product(k))
            if len(waiting) > 1:
                held.append(turn(waiting.pop(0)))
        while waiting:
            held.append(turn(waiting.pop(0)))
        for x in held:
            done += leave(x)
        return done

    def put(block, line, col):
        result[pl.ds(block * blocks * LINES + line, blocks, stride=LINES), :] = col

    pairs = [(j, q) for j in range(copies) for q in range(SHARE)]
    size, part = len(pairs) * blocks, SHARE * blocks
    re, im = spectrum(
        [j * blocks * LINES + q for j, q in pairs]
        + [j * blocks * LINES + SHARE + q for j, q in pairs]
        + [q * blocks * LINES + 2 * SHARE for q in range(SHARE)]
    )
    v_re, v_im, g_re, g_im = re[:size], im[:size], re[size : 2 * size], im[size : 2 * size]
    h_re = jnp.concatenate([re[2 * size :]] * copies, axis=0)
    h_im = jnp.concatenate([im[2 * size :]] * copies, axis=0)
    f_re, f_im = v_re * g_re + v_im * g_im, v_re * g_im - v_im * g_re
    f_re = sum(f_re[j * part : (j + 1) * part] for j in range(copies))
    f_im = sum(f_im[j * part : (j + 1) * part] for j in range(copies))
    cols = signal(
        jnp.concatenate([h_re * v_re - h_im * v_im, h_re * g_re + h_im * g_im, f_re], axis=0),
        jnp.concatenate([h_re * v_im + h_im * v_re, h_re * g_im - h_im * g_re, f_im], axis=0),
    )
    for k, (j, q) in enumerate(pairs):
        put(j, q, cols[k])
        put(j, SHARE + q, cols[len(pairs) + k])
    for j in range(SHARE):
        for line in range(2 * SHARE, LINES):
            put(j, line, cols[2 * len(pairs) + j])
    out_ref[...] = result[: out_ref.shape[0], :].astype(BF16)


def finish_kernel(
    values_ref, gates_ref, grad_ref, skip_ref, in_ref, value_out, gate_out, filter_out, wide, value, gate, taps, sems
):
    pairs = in_ref.shape[0] // LINES
    wide[: in_ref.shape[0], :] = in_ref[...].astype(F32)
    copies = []

    def send(src, dst):
        copy = pltpu.make_async_copy(src, dst, sems.at[len(copies)])
        copy.start()
        copies.append(copy)

    taps[...] = wide[pl.ds(2 * SHARE, pairs, stride=LINES), :].T
    send(taps, filter_out)
    for q in range(SHARE):
        cut = slice(q * pairs, (q + 1) * pairs)
        grad, skip = grad_ref[:, cut], skip_ref[:, cut]
        conv = wide[pl.ds(q, pairs, stride=LINES), :].T
        gate[:, cut] = (grad * (conv + skip * values_ref[:, cut].astype(F32))).astype(BF16)
    send(gate, gate_out)
    for q in range(SHARE):
        cut = slice(q * pairs, (q + 1) * pairs)
        grad, skip = grad_ref[:, cut], skip_ref[:, cut]
        back = wide[pl.ds(SHARE + q, pairs, stride=LINES), :].T
        gate_term = (grad * gates_ref[:, cut].astype(F32)).astype(BF16).astype(F32)
        value[:, cut] = (back + skip * gate_term).astype(BF16)
    send(value, value_out)
    for copy in copies:
        copy.wait()


def call(kernel, out_shape, args, scratch, specs=None, limit=48, out=VMEM):
    return pl.pallas_call(
        kernel,
        out_shape=out_shape,
        in_specs=specs or [VMEM] * len(args),
        out_specs=jax.tree.map(lambda _: out, out_shape),
        scratch_shapes=scratch,
        compiler_params=pltpu.CompilerParams(vmem_limit_bytes=limit * 1024 * 1024),
    )(*args)


def spare(x):
    return pltpu.VMEM((x.shape[0] + 16, x.shape[1]), F32)


def exchange(x):
    shaped = x.reshape(lax.axis_size("chan") * lax.axis_size("seq"), -1, 2, x.shape[1])
    moved = lax.all_to_all(shaped, ("chan", "seq"), split_axis=0, concat_axis=0, tiled=True)
    return moved.reshape(x.shape)


def transform(held, blocks):
    rows = held.shape[1]
    consts = tables(blocks, rows)
    return call(
        spectra_kernel,
        jax.ShapeDtypeStruct(held.shape, BF16),
        (held, *consts),
        [spare(held), spare(held)],
    )


def local(values, gates, grad_out, filter_raw, skip_gain):
    rows, width = values.shape
    blocks = lax.axis_size("seq")
    pairs = blocks * lax.axis_size("chan")
    rank = lax.axis_index("chan").astype(jnp.int32).reshape(1)
    scalar = pl.BlockSpec(memory_space=pltpu.SMEM)
    sent = jax.ShapeDtypeStruct((pairs * LINES, rows), BF16)
    sent = call(
        pack_kernel,
        pltpu.VMEM(sent.shape, BF16),
        (rank, values, gates, grad_out, filter_raw),
        [
            pltpu.VMEM((rows, width), BF16),
            pltpu.VMEM((rows, width), BF16),
            pltpu.VMEM((rows, width), F32),
            pltpu.VMEM((rows, width), BF16),
            spare(sent),
            pltpu.SemaphoreType.DMA((4,)),
        ],
        [scalar] + [pl.BlockSpec(memory_space=pltpu.HBM)] * 4,
        limit=57,
    )
    back = exchange(transform(exchange(sent), blocks))
    shape = jax.ShapeDtypeStruct((rows, width), BF16)
    return call(
        finish_kernel,
        (shape, shape, jax.ShapeDtypeStruct((rows, width // lax.axis_size("chan")), F32)),
        (values, gates, grad_out, skip_gain[None, :], back),
        [
            spare(back),
            pltpu.VMEM((rows, width), BF16),
            pltpu.VMEM((rows, width), BF16),
            pltpu.VMEM((rows, pairs), F32),
            pltpu.SemaphoreType.DMA((3,)),
        ],
        out=pl.BlockSpec(memory_space=pltpu.HBM),
    )


def solution(mesh):
    in_specs = (P("seq", "chan"), P("seq", "chan"), P("seq", "chan"), P("seq", None), P("chan"))
    out_specs = (P("seq", "chan"), P("seq", "chan"), P("seq", "chan"))
    return jax.shard_map(local, mesh=mesh, in_specs=in_specs, out_specs=out_specs, check_vma=False)
```

```python
import math

import jax
import jax.numpy as jnp
import numpy as np
from jax import lax
from jax.experimental import pallas as pl
from jax.experimental.pallas import tpu as pltpu
from jax.sharding import PartitionSpec as P

F32 = jnp.float32
BF16 = jnp.bfloat16
VMEM = pl.BlockSpec(memory_space=pltpu.VMEM)
SHARE = 4
PIECES = 4
LINES = 10


def split_pair(table):
    high = table.astype(np.float32).astype(jnp.bfloat16)
    low = (table - high.astype(np.float64)).astype(np.float32).astype(jnp.bfloat16)
    return high, low


def tables(blocks, rows):
    period = 2 * blocks * rows
    scale = 2.0 / period / math.sqrt(blocks * rows)
    half = np.arange(blocks) + 0.5
    block_angle = 2.0 * np.pi / (2 * blocks) * np.outer(half, np.arange(blocks))
    enter = np.concatenate([np.cos(block_angle), -np.sin(block_angle)], axis=0)
    leave = np.concatenate([np.cos(block_angle), -np.sin(block_angle)], axis=0).T * scale
    turn = 2.0 * np.pi / period * np.outer(half, np.arange(rows))
    row_angle = 2.0 * np.pi / rows * np.outer(np.arange(rows), np.arange(rows))
    row_cos, row_sin = np.cos(row_angle), np.sin(row_angle)
    forward = np.block([[row_cos, -row_sin], [row_sin, row_cos]])
    inverse = np.block([[row_cos, row_sin], [-row_sin, row_cos]])
    enter_high, enter_low = split_pair(enter)
    leave_high, leave_low = split_pair(leave)
    wide = [
        np.concatenate([high, low, high], axis=0)
        for high, low in (split_pair(forward), split_pair(inverse))
    ]
    wide.append(np.block([[leave_high, leave_high], [leave_low, np.zeros_like(leave_low)]]))
    turns = np.concatenate([np.cos(turn), np.sin(turn)], axis=0).astype(np.float32)
    return np.concatenate([enter_high, enter_low], axis=1), np.concatenate(wide, axis=0), turns


def split_value(x):
    high = x.astype(BF16)
    return high, (x - high.astype(F32)).astype(BF16)


def dot(a, b):
    return jnp.dot(a, b, preferred_element_type=F32)


def triple(x, axis):
    high, low = split_value(x)
    return jnp.concatenate([high, high, low], axis=axis)


def dot_rows(x, table):
    size = x.shape[0] // PIECES
    parts = [dot(triple(x[k * size : (k + 1) * size], 1), table) for k in range(PIECES)]
    return jnp.concatenate(parts, axis=0)


def pack_kernel(rank_ref, values_ref, gates_ref, grad_ref, filter_ref, out_ref, values, gates, grad, taps, rows_ref, sems):
    pairs = out_ref.shape[0] // LINES
    cut = pl.ds(pl.multiple_of(rank_ref[0] * pairs, pairs), pairs)
    moves = (
        (values_ref, values),
        (filter_ref.at[:, cut], taps),
        (gates_ref, gates),
        (grad_ref, grad),
    )
    copies = [pltpu.make_async_copy(src, dst, sems.at[k]) for k, (src, dst) in enumerate(moves)]
    for copy in copies:
        copy.start()

    def put(line, rows):
        rows_ref[pl.ds(line, pairs, stride=LINES), :] = rows

    def place(part, first):
        turned = part.T
        for q in range(SHARE):
            put(first + q, turned[q * pairs : (q + 1) * pairs, :])

    copies[0].wait()
    place(values[...].astype(F32), 0)
    copies[1].wait()
    own = taps[...].astype(F32).T
    for line in range(2 * SHARE, LINES):
        put(line, own)
    copies[2].wait()
    copies[3].wait()
    gate_term = (grad[...] * gates[...].astype(F32)).astype(BF16).astype(F32)
    place(gate_term, SHARE)
    out_ref[...] = rows_ref[: out_ref.shape[0], :].astype(BF16)


def spectra_kernel(
    in_ref, enter_ref, table_ref, turn_ref, out_ref, wide, result
):
    blocks, rows = turn_ref.shape[0] // 2, turn_ref.shape[1]
    deep = 6 * rows
    copies = in_ref.shape[0] // (blocks * LINES)
    cos_t, sin_t = turn_ref[:blocks, :], turn_ref[blocks:, :]
    wide[: in_ref.shape[0], :] = in_ref[...].astype(F32)

    def spectrum(starts):
        table = table_ref[:deep, :]
        step = len(starts) // PIECES

        def turn(first):
            cols = [wide[pl.ds(start, blocks, stride=LINES), :] for start in starts[first : first + step]]
            joined = jnp.concatenate(cols, axis=1).astype(BF16)
            mixed = dot(enter_ref[...], jnp.concatenate([joined, joined], axis=0))
            turned = []
            for c in range(step):
                re = mixed[:blocks, c * rows : (c + 1) * rows]
                im = mixed[blocks:, c * rows : (c + 1) * rows]
                turned.append(
                    jnp.concatenate([re * cos_t + im * sin_t, im * cos_t - re * sin_t], axis=1)
                )
            return triple(jnp.concatenate(turned, axis=0), 1)

        full = []
        ready = turn(0)
        for first in range(0, len(starts), step):
            ahead = turn(first + step) if first + step < len(starts) else None
            full.append(dot(ready, table))
            ready = ahead
        full = jnp.concatenate(full, axis=0)
        return full[:, :rows], full[:, rows:]

    def signal(re, im):
        table = table_ref[deep : 2 * deep, :]
        size = re.shape[0] // 4
        starts = list(range(0, re.shape[0], size))

        def product(k):
            return dot(triple(jnp.concatenate([re[k : k + size], im[k : k + size]], axis=1), 1), table)

        def turn(full):
            cols = []
            for c in range(0, size, blocks):
                x, y = full[c : c + blocks, :rows], full[c : c + blocks, rows:]
                cols.append(jnp.concatenate([x * cos_t - y * sin_t, x * sin_t + y * cos_t], axis=0))
            return jnp.concatenate(split_value(jnp.concatenate(cols, axis=1)), axis=0)

        waiting, done = [], []

        def leave(x):
            both = dot(table_ref[2 * deep :, :], x)
            mixed = both[:blocks] + both[blocks:]
            return [mixed[:, c : c + rows] for c in range(0, mixed.shape[1], rows)]

        held = []
        for k in starts:
            waiting.append(product(k))
            if len(waiting) > 1:
                held.append(turn(waiting.pop(0)))
        while waiting:
            held.append(turn(waiting.pop(0)))
        for x in held:
            done += leave(x)
        return done

    def put(block, line, col):
        result[pl.ds(block * blocks * LINES + line, blocks, stride=LINES), :] = col

    pairs = [(j, q) for j in range(copies) for q in range(SHARE)]
    size, part = len(pairs) * blocks, SHARE * blocks
    re, im = spectrum(
        [j * blocks * LINES + q for j, q in pairs]
        + [j * blocks * LINES + SHARE + q for j, q in pairs]
        + [q * blocks * LINES + 2 * SHARE for q in range(SHARE)]
    )
    v_re, v_im, g_re, g_im = re[:size], im[:size], re[size : 2 * size], im[size : 2 * size]
    h_re = jnp.concatenate([re[2 * size :]] * copies, axis=0)
    h_im = jnp.concatenate([im[2 * size :]] * copies, axis=0)
    f_re, f_im = v_re * g_re + v_im * g_im, v_re * g_im - v_im * g_re
    f_re = sum(f_re[j * part : (j + 1) * part] for j in range(copies))
    f_im = sum(f_im[j * part : (j + 1) * part] for j in range(copies))
    cols = signal(
        jnp.concatenate([h_re * v_re - h_im * v_im, h_re * g_re + h_im * g_im, f_re], axis=0),
        jnp.concatenate([h_re * v_im + h_im * v_re, h_re * g_im - h_im * g_re, f_im], axis=0),
    )
    for k, (j, q) in enumerate(pairs):
        put(j, q, cols[k])
        put(j, SHARE + q, cols[len(pairs) + k])
    for j in range(SHARE):
        for line in range(2 * SHARE, LINES):
            put(j, line, cols[2 * len(pairs) + j])
    out_ref[...] = result[: out_ref.shape[0], :].astype(BF16)


def finish_kernel(
    values_ref, gates_ref, grad_ref, skip_ref, in_ref, value_out, gate_out, filter_out, wide, value, gate, taps, sems
):
    pairs = in_ref.shape[0] // LINES
    wide[: in_ref.shape[0], :] = in_ref[...].astype(F32)
    copies = []

    def send(src, dst):
        copy = pltpu.make_async_copy(src, dst, sems.at[len(copies)])
        copy.start()
        copies.append(copy)

    taps[...] = wide[pl.ds(2 * SHARE, pairs, stride=LINES), :].T
    send(taps, filter_out)
    for q in range(SHARE):
        cut = slice(q * pairs, (q + 1) * pairs)
        grad, skip = grad_ref[:, cut], skip_ref[:, cut]
        conv = wide[pl.ds(q, pairs, stride=LINES), :].T
        gate[:, cut] = (grad * (conv + skip * values_ref[:, cut].astype(F32))).astype(BF16)
    send(gate, gate_out)
    for q in range(SHARE):
        cut = slice(q * pairs, (q + 1) * pairs)
        grad, skip = grad_ref[:, cut], skip_ref[:, cut]
        back = wide[pl.ds(SHARE + q, pairs, stride=LINES), :].T
        gate_term = (grad * gates_ref[:, cut].astype(F32)).astype(BF16).astype(F32)
        value[:, cut] = (back + skip * gate_term).astype(BF16)
    send(value, value_out)
    for copy in copies:
        copy.wait()


def call(kernel, out_shape, args, scratch, specs=None, limit=48, out=VMEM):
    return pl.pallas_call(
        kernel,
        out_shape=out_shape,
        in_specs=specs or [VMEM] * len(args),
        out_specs=jax.tree.map(lambda _: out, out_shape),
        scratch_shapes=scratch,
        compiler_params=pltpu.CompilerParams(vmem_limit_bytes=limit * 1024 * 1024),
    )(*args)


def spare(x):
    return pltpu.VMEM((x.shape[0] + 16, x.shape[1]), F32)


def exchange(x):
    shaped = x.reshape(lax.axis_size("chan") * lax.axis_size("seq"), -1, 2, x.shape[1])
    moved = lax.all_to_all(shaped, ("chan", "seq"), split_axis=0, concat_axis=0, tiled=True)
    return moved.reshape(x.shape)


def transform(held, blocks):
    rows = held.shape[1]
    consts = tables(blocks, rows)
    return call(
        spectra_kernel,
        jax.ShapeDtypeStruct(held.shape, BF16),
        (held, *consts),
        [spare(held), spare(held)],
    )


def local(values, gates, grad_out, filter_raw, skip_gain):
    rows, width = values.shape
    blocks = lax.axis_size("seq")
    pairs = blocks * lax.axis_size("chan")
    rank = lax.axis_index("chan").astype(jnp.int32).reshape(1)
    scalar = pl.BlockSpec(memory_space=pltpu.SMEM)
    sent = jax.ShapeDtypeStruct((pairs * LINES, rows), BF16)
    sent = call(
        pack_kernel,
        pltpu.VMEM(sent.shape, BF16),
        (rank, values, gates, grad_out, filter_raw),
        [
            pltpu.VMEM((rows, width), BF16),
            pltpu.VMEM((rows, width), BF16),
            pltpu.VMEM((rows, width), F32),
            pltpu.VMEM((rows, pairs), BF16),
            spare(sent),
            pltpu.SemaphoreType.DMA((4,)),
        ],
        [scalar] + [pl.BlockSpec(memory_space=pltpu.HBM)] * 4,
        limit=57,
    )
    back = exchange(transform(exchange(sent), blocks))
    shape = jax.ShapeDtypeStruct((rows, width), BF16)
    return call(
        finish_kernel,
        (shape, shape, jax.ShapeDtypeStruct((rows, width // lax.axis_size("chan")), F32)),
        (values, gates, grad_out, skip_gain[None, :], back),
        [
            spare(back),
            pltpu.VMEM((rows, width), BF16),
            pltpu.VMEM((rows, width), BF16),
            pltpu.VMEM((rows, pairs), F32),
            pltpu.SemaphoreType.DMA((3,)),
        ],
        out=pl.BlockSpec(memory_space=pltpu.HBM),
    )


def solution(mesh):
    in_specs = (P("seq", "chan"), P("seq", "chan"), P("seq", "chan"), P("seq", None), P("chan"))
    out_specs = (P("seq", "chan"), P("seq", "chan"), P("seq", "chan"))
    return jax.shard_map(local, mesh=mesh, in_specs=in_specs, out_specs=out_specs, check_vma=False)
```
